512 devices in a mesh: rep: 32 (over x, y), fsdp: 16 (over z, core).
Axes of the slice: x: 4, y: 8, z: 8, core: 2. Of those that a mesh axis runs over, the one named last changes fastest.
Arguments:
- grads: bfloat16 [8, 576, 2048], P(None, 'fsdp')
- momentum: float32 [32, 576, 2048], P('rep', 'fsdp')
- owners: int32 [8], replicated, may hold values from 0 to 31, as said below
Outputs:
- update: bfloat16 [8, 576, 2048], P(None, 'fsdp')
- new_momentum: float32 [32, 576, 2048], P('rep', 'fsdp')
The draws below stay inside these ranges and needn't reach their ends.
Inputs may be any that keep to these rules, and one draw needn't show every extreme that they name: The owners are distinct; owner 0 and the last replica group always appear.
All inputs are finite; a program needn't handle non-finite values.
Results may differ from the reference program's by a relative error of at most 0.001.
Values may be sent and summed in bfloat16 or wider, within the bound.
No kernel may reach another device: no remote copies, remote signals or barrier semaphores. Data moves between devices by JAX's collectives and lax.ppermute only.
A program may use at most 64 MiB of HBM per device.

```python
import math
import jax
import jax.numpy as jnp
from jax import lax

ROWS = 576
COLS = 2048
MATS = 8
ITERS = 3
N_REP = 32


def rough_parts(key, count):
    k_base, k_rows, k_cols = jax.random.split(key, 3)
    noise_base = jax.random.normal(k_base, (count, ROWS, COLS), jnp.float32)
    rising = 1.0 + 2.0 * jnp.arange(ROWS, dtype=jnp.float32) / max(ROWS - 1, 1)
    row_scale = rising[None, :, None] * jnp.exp(jax.random.uniform(k_rows, (count, ROWS, 1), jnp.float32) * math.log(10.0))
    col_scale = jnp.exp(jax.random.uniform(k_cols, (count, 1, COLS), jnp.float32) * math.log(10.0))
    rough_values = noise_base * row_scale * col_scale
    return rough_values


def draw_grads(key, part):
    key = jax.random.fold_in(key, 5)
    rough_values = rough_parts(key, MATS)
    values = 0.05 * rough_values
    return values.astype(jnp.bfloat16)


def draw_momentum(key, part):
    key = jax.random.fold_in(key, 7)
    rough_values = rough_parts(key, N_REP)
    values = 0.05 * rough_values
    return values.astype(jnp.float32)


def draw_owners(key, part):
    key = jax.random.fold_in(key, 11)
    k_middle, k_order = jax.random.split(key, 2)
    end_points = jnp.array([0, N_REP - 1], dtype=jnp.int32)
    middle_ids = 1 + jax.random.permutation(k_middle, N_REP - 2)[:MATS - 2].astype(jnp.int32)
    chosen = jnp.concatenate([end_points, middle_ids])
    shuffle = jax.random.permutation(k_order, MATS)
    return chosen[shuffle].astype(jnp.int32)


def setup_inputs(seed: int = 0) -> dict:
    key_of = jax.random.split(jax.random.key(seed), 4)
    return {
        "grads": draw_grads(jax.random.fold_in(key_of[3], 71), 0),
        "momentum": draw_momentum(jax.random.fold_in(key_of[3], 71), 0),
        "owners": draw_owners(jax.random.fold_in(key_of[3], 71), 0),
    }


EPSILON = 1e-07
MOMENTUM_BETA = 0.95
QUINTIC_A = 3.4445
QUINTIC_B = -4.775
QUINTIC_C = 2.0315

def matmul(left, right):
    return jnp.dot(left, right, precision=lax.Precision.HIGHEST, preferred_element_type=jnp.float32)

def newton_schulz(steered):
    iterate = steered / (jnp.sqrt(jnp.sum(steered * steered)) + EPSILON)
    for iteration in range(ITERS):
        gram_matrix = matmul(iterate, iterate.T)
        polynomial = QUINTIC_B * gram_matrix + QUINTIC_C * matmul(gram_matrix, gram_matrix)
        iterate = QUINTIC_A * iterate + matmul(polynomial, iterate)
    return iterate

def reference(grads, momentum, owners):
    factor = 0.2 * math.sqrt(max(ROWS, COLS))
    renewed = momentum
    updates = []
    for matrix_index in range(MATS):
        owner_id = owners[matrix_index].astype(jnp.int32)
        gradient = grads[matrix_index].astype(jnp.float32)
        held_state = lax.dynamic_index_in_dim(momentum, owner_id, 0, keepdims=False)
        fresh_state = MOMENTUM_BETA * held_state + gradient
        renewed = lax.dynamic_update_index_in_dim(renewed, fresh_state, owner_id, 0)
        steered = gradient + MOMENTUM_BETA * fresh_state
        updates.append((factor * newton_schulz(steered)).astype(jnp.bfloat16))
    return (jnp.stack(updates), renewed)
```

```python
import math

import jax
import jax.numpy as jnp
from jax import lax
from jax.experimental import pallas as pl
from jax.experimental.pallas import tpu as pltpu
from jax.sharding import PartitionSpec as P

ROWS = 576
COLS = 2048
MATS = 8
ITERS = 3
N_FSDP = 16
OWN = ROWS // N_FSDP
PAD = 40
TALL = PAD * N_FSDP
NX, NY = 4, 8
N_REP = NX * NY
HALF = OWN // 2
CHUNK = 512

EPSILON = 1e-07
MOMENTUM_BETA = 0.95
QUINTIC_A = 3.4445
QUINTIC_B = -4.775
QUINTIC_C = 2.0315

f32, bf16 = jnp.float32, jnp.bfloat16


def split(value):
    high = value.astype(bf16)
    low = (value - high.astype(f32)).astype(bf16)
    return high, low


def product(left, right):
    lh, ll = left
    rh, rl = right
    small = jnp.dot(lh, rl, preferred_element_type=f32) + jnp.dot(ll, rh, preferred_element_type=f32)
    return small + jnp.dot(lh, rh, preferred_element_type=f32)


def product_nt(left, right):
    lh, ll = left
    rh, rl = right

    def dot(a, b):
        return lax.dot_general(a, b, (((1,), (1,)), ((), ())), preferred_element_type=f32)

    return (dot(lh, rl) + dot(ll, rh)) + dot(lh, rh)


def orthogonal_kernel(me_ref, s_ref, u_ref, high_ref, low_ref, gram_ref, rows_ref):
    step = pl.program_id(0)
    steps = pl.num_programs(0)
    high, low = split(s_ref[...])
    high_ref[step] = high
    low_ref[step] = low
    part = product_nt((high, low), (high, low))

    @pl.when(step == 0)
    def _():
        gram_ref[...] = part

    @pl.when(step > 0)
    def _():
        gram_ref[...] += part

    @pl.when(step == steps - 1)
    def _():
        row = lax.broadcasted_iota(jnp.int32, (TALL, TALL), 0)
        col = lax.broadcasted_iota(jnp.int32, (TALL, TALL), 1)
        diagonal = row == col
        gram = gram_ref[...]
        total = jnp.sum(jnp.where(diagonal, gram, 0.0), axis=(0, 1), keepdims=True)
        inverse = 1.0 / (jnp.sqrt(total) + EPSILON)
        start = pl.multiple_of(me_ref[0] * PAD, 8)
        mine = pl.ds(start, PAD)

        def poly(gram, square):
            return jnp.where(diagonal, QUINTIC_A, 0.0) + QUINTIC_B * gram + QUINTIC_C * square

        g0 = gram * inverse * inverse
        g0s = split(g0)
        q1 = poly(g0, product(g0s, g0s))
        q1s = split(q1)
        g1 = product(split(product(q1s, g0s)), q1s)
        g1s = split(g1)
        q2 = poly(g1, product(g1s, g1s))
        q2s = split(q2)
        rows_ref[...] = q2
        q2_mine = rows_ref[mine, :]
        g2_mine = product(split(product(split(q2_mine), g1s)), q2s)
        square = product(split(g2_mine), q2s)
        square = product(split(product(split(square), g1s)), q2s)
        own = lax.broadcasted_iota(jnp.int32, (PAD, TALL), 0) + start
        here = lax.broadcasted_iota(jnp.int32, (PAD, TALL), 1)
        q3_mine = jnp.where(own == here, QUINTIC_A, 0.0) + QUINTIC_B * g2_mine + QUINTIC_C * square
        mix = split(product(split(product(split(q3_mine), q2s)), q1s))
        factor = 0.2 * math.sqrt(max(ROWS, COLS))
        for part in range(COLS // CHUNK):
            update = product(mix, (high_ref[part], low_ref[part])) * inverse * factor
            for block in range(CHUNK // 128):
                lane = part * (CHUNK // 128) + block
                iy, left = lane // 2, lane % 2
                for half in range(2):
                    ix = left * 2 + half
                    piece = update[half * HALF : (half + 1) * HALF, block * 128 : (block + 1) * 128]
                    u_ref[ix * NY + iy] = piece.astype(bf16)


def orthogonal_rows(position, whole):
    return pl.pallas_call(
        orthogonal_kernel,
        grid=(COLS // CHUNK,),
        out_shape=jax.ShapeDtypeStruct((N_REP, HALF, 128), bf16),
        in_specs=[
            pl.BlockSpec(memory_space=pltpu.SMEM),
            pl.BlockSpec((TALL, CHUNK), lambda i: (0, i)),
        ],
        out_specs=pl.BlockSpec((N_REP, HALF, 128), lambda i: (0, 0, 0)),
        scratch_shapes=[
            pltpu.VMEM((COLS // CHUNK, TALL, CHUNK), bf16),
            pltpu.VMEM((COLS // CHUNK, TALL, CHUNK), bf16),
            pltpu.VMEM((TALL, TALL), f32),
            pltpu.VMEM((TALL, TALL), f32),
        ],
        compiler_params=pltpu.CompilerParams(vmem_limit_bytes=48 * 1024 * 1024),
    )(position, whole)


def assemble_kernel(my_y_ref, *refs):
    out_ref = refs[-1]
    for distance in range(NY):
        lane = lax.rem(my_y_ref[0] + NY - distance, NY) * 256
        for left in range(2):
            upper = refs[distance][2 * left].astype(f32)
            lower = refs[distance][2 * left + 1].astype(f32)
            lanes = pl.ds(pl.multiple_of(lane + left * 128, 128), 128)
            for mat in range(MATS):
                span = slice(mat * HALF, (mat + 1) * HALF)
                block = jnp.concatenate([upper[span], lower[span]], axis=0)
                out_ref[mat, :, lanes] = block.astype(bf16)


def assemble(my_y, parts):
    return pl.pallas_call(
        assemble_kernel,
        out_shape=jax.ShapeDtypeStruct((MATS, OWN, COLS), bf16),
        in_specs=[pl.BlockSpec(memory_space=pltpu.SMEM)] + [pl.BlockSpec(memory_space=pltpu.VMEM)] * NY,
        out_specs=pl.BlockSpec(memory_space=pltpu.VMEM),
        compiler_params=pltpu.CompilerParams(vmem_limit_bytes=32 * 1024 * 1024),
    )(my_y, *parts)


def shift_x(value, distance):
    pairs = [(x * NY + y, (x + distance) % NX * NY + y) for x in range(NX) for y in range(NY)]
    return lax.ppermute(value, "rep", pairs)


def shift_y(value, distance):
    pairs = [(x * NY + y, x * NY + (y + distance) % NY) for x in range(NX) for y in range(NY)]
    return lax.ppermute(value, "rep", pairs)


def deliver(pieces, owners):
    group = lax.axis_index("rep")
    my_x, my_y = group // NY, group % NY
    arrived = lax.all_to_all(pieces, "rep", split_axis=0, concat_axis=0, tiled=True)
    chosen = jnp.take(arrived, owners, axis=0, mode="clip").reshape(MATS * HALF, 128)
    along_x = [chosen] + [shift_x(chosen, d) for d in range(1, NX)]
    relative = jnp.stack(along_x[::-1] + along_x[:0:-1])
    absolute = lax.dynamic_slice_in_dim(relative, NX - 1 - my_x, NX, axis=0)
    along_y = [absolute] + [shift_y(absolute, d) for d in range(1, NY)]
    return assemble(my_y.astype(jnp.int32)[None], along_y)


def shards(grads, momentum, owners):
    my_group = lax.axis_index("rep")
    positions = jnp.arange(MATS, dtype=jnp.int32)
    is_mine = owners == my_group
    owns_one = jnp.any(is_mine)
    chosen = jnp.sum(jnp.where(is_mine, positions, 0))
    gradient = lax.dynamic_index_in_dim(grads, chosen, 0, keepdims=False).astype(f32)
    held_state = momentum[0]
    renewed = jnp.where(owns_one, MOMENTUM_BETA * held_state + gradient, held_state)
    steered = gradient + MOMENTUM_BETA * renewed
    padded = jnp.pad(steered, ((0, PAD - OWN), (0, 0)))
    whole = lax.all_gather(padded, "fsdp", axis=0, tiled=True)
    position = lax.axis_index("fsdp").astype(jnp.int32)[None]
    pieces = orthogonal_rows(position, whole)
    update = deliver(pieces, owners)
    return (update, renewed[None])


def solution(mesh):
    in_specs = (P(None, "fsdp", None), P("rep", "fsdp", None), P())
    out_specs = (P(None, "fsdp", None), P("rep", "fsdp", None))
    return jax.shard_map(shards, mesh=mesh, in_specs=in_specs, out_specs=out_specs, check_vma=False)
```

```python
import math

import jax
import jax.numpy as jnp
from jax import lax
from jax.experimental import pallas as pl
from jax.experimental.pallas import tpu as pltpu
from jax.sharding import PartitionSpec as P

ROWS = 576
COLS = 2048
MATS = 8
ITERS = 3
N_FSDP = 16
OWN = ROWS // N_FSDP
PAD = 40
TALL = PAD * N_FSDP
NX, NY = 4, 8
N_REP = NX * NY
HALF = OWN // 2
CHUNK = 512

EPSILON = 1e-07
MOMENTUM_BETA = 0.95
QUINTIC_A = 3.4445
QUINTIC_B = -4.775
QUINTIC_C = 2.0315

f32, bf16 = jnp.float32, jnp.bfloat16


def split(value):
    high = value.astype(bf16)
    low = (value - high.astype(f32)).astype(bf16)
    return high, low


def dot(left, right):
    return jnp.dot(left, right, preferred_element_type=f32)


def dot_nt(left, right):
    return lax.dot_general(left, right, (((1,), (1,)), ((), ())), preferred_element_type=f32)


def product(left, right):
    (lh, ll), (rh, rl) = left, right
    return (dot(lh, rl) + dot(ll, rh)) + dot(lh, rh)


def square(halves):
    high, low = halves
    cross = dot(high, low)
    return (cross + cross.T) + dot(high, high)


def thin_product(rows, halves):
    high, low = halves
    kept = rows.astype(bf16).astype(f32)
    stacked = jnp.concatenate([kept, rows - kept], axis=0).astype(bf16)
    first = dot(stacked, high)
    second = dot(stacked, low)
    return first[:PAD] + (first[PAD:] + second[:PAD])


def orthogonal_kernel(me_ref, s_hbm, u_ref, s_ref, high_ref, low_ref, rows_ref, sems):
    chunks = COLS // CHUNK

    def fetch(part):
        lanes = pl.ds(part * CHUNK, CHUNK)
        return pltpu.make_async_copy(s_hbm.at[:, lanes], s_ref.at[part], sems.at[part])

    for part in range(chunks):
        fetch(part).start()
    gram = None
    cross = None
    for part in range(chunks):
        fetch(part).wait()
        high, low = split(s_ref[part])
        high_ref[part] = high
        low_ref[part] = low
        more_cross, more = dot_nt(high, low), dot_nt(high, high)
        cross = more_cross if part == 0 else cross + more_cross
        gram = more if part == 0 else gram + more
    gram = gram + (cross + cross.T)

    row = lax.broadcasted_iota(jnp.int32, (TALL, TALL), 0)
    col = lax.broadcasted_iota(jnp.int32, (TALL, TALL), 1)
    diagonal = row == col
    total = jnp.sum(jnp.where(diagonal, gram, 0.0), axis=(0, 1), keepdims=True)
    inverse = 1.0 / (jnp.sqrt(total) + EPSILON)
    start = pl.multiple_of(me_ref[0] * PAD, 8)

    def poly(gram, squared):
        return jnp.where(diagonal, QUINTIC_A, 0.0) + QUINTIC_B * gram + QUINTIC_C * squared

    g0 = gram * inverse * inverse
    g0s = split(g0)
    q1s = split(poly(g0, square(g0s)))
    g1 = product(g0s, split(square(q1s)))
    g1s = split(g1)
    q2 = poly(g1, square(g1s))
    q2s = split(q2)
    rows_ref[...] = q2
    mixed = thin_product(rows_ref[pl.ds(start, PAD), :], q1s)

    def by_g2(rows):
        return thin_product(thin_product(thin_product(rows, g1s), q2s), q2s)

    once = by_g2(mixed)
    twice = by_g2(once)
    mixed = QUINTIC_A * mixed + QUINTIC_B * once + QUINTIC_C * twice
    factor = 0.2 * math.sqrt(max(ROWS, COLS))
    for part in range(chunks):
        update = thin_product(mixed, (high_ref[part], low_ref[part])) * inverse * factor
        for block in range(CHUNK // 128):
            lane = part * (CHUNK // 128) + block
            iy, left = lane // 2, lane % 2
            for half in range(2):
                ix = left * 2 + half
                piece = update[half * HALF : (half + 1) * HALF, block * 128 : (block + 1) * 128]
                u_ref[ix * NY + iy] = piece.astype(bf16)


def orthogonal_rows(position, whole):
    chunks = COLS // CHUNK
    return pl.pallas_call(
        orthogonal_kernel,
        out_shape=jax.ShapeDtypeStruct((N_REP, HALF, 128), bf16),
        in_specs=[
            pl.BlockSpec(memory_space=pltpu.SMEM),
            pl.BlockSpec(memory_space=pltpu.HBM),
        ],
        out_specs=pl.BlockSpec(memory_space=pltpu.VMEM),
        scratch_shapes=[
            pltpu.VMEM((chunks, TALL, CHUNK), f32),
            pltpu.VMEM((chunks, TALL, CHUNK), bf16),
            pltpu.VMEM((chunks, TALL, CHUNK), bf16),
            pltpu.VMEM((TALL, TALL), f32),
            pltpu.SemaphoreType.DMA((chunks,)),
        ],
        compiler_params=pltpu.CompilerParams(vmem_limit_bytes=48 * 1024 * 1024),
    )(position, whole)


def choose_kernel(owners_ref, arrived_ref, out_ref, rows_ref):
    for mat in range(MATS):
        rows_ref[pl.ds(mat, HALF, stride=MATS), :] = arrived_ref[owners_ref[mat]].astype(f32)
    rows = rows_ref[...].astype(bf16)
    for copy in range(NY):
        out_ref[copy] = rows


def choose(owners, arrived):
    return pl.pallas_call(
        choose_kernel,
        out_shape=jax.ShapeDtypeStruct((NY, HALF * MATS, 128), bf16),
        in_specs=[pl.BlockSpec(memory_space=pltpu.SMEM), pl.BlockSpec(memory_space=pltpu.VMEM)],
        out_specs=pl.BlockSpec(memory_space=pltpu.VMEM),
        scratch_shapes=[pltpu.VMEM((HALF * MATS, 128), f32)],
        compiler_params=pltpu.CompilerParams(vmem_limit_bytes=16 * 1024 * 1024),
    )(owners, arrived)


def assemble_kernel(parts_ref, out_hbm, rows_ref, sems):
    def store(half):
        rows = pl.ds(half * HALF, HALF)
        return pltpu.make_async_copy(rows_ref.at[rows], out_hbm.at[rows], sems.at[half])

    for half in range(2):
        for iy in range(NY):
            for left in range(2):
                lane = (iy * 2 + left) * 128
                piece = parts_ref[2 * left + half, iy * HALF : (iy + 1) * HALF]
                rows_ref[half * HALF : (half + 1) * HALF, :, lane : lane + 128] = piece
        store(half).start()
    for half in range(2):
        store(half).wait()


def assemble(parts):
    return pl.pallas_call(
        assemble_kernel,
        out_shape=pltpu.HBM((OWN, MATS, COLS), bf16),
        in_specs=[pl.BlockSpec(memory_space=pltpu.VMEM)],
        out_specs=pl.BlockSpec(memory_space=pltpu.HBM),
        scratch_shapes=[pltpu.VMEM((OWN, MATS, COLS), bf16), pltpu.SemaphoreType.DMA((2,))],
        compiler_params=pltpu.CompilerParams(vmem_limit_bytes=32 * 1024 * 1024),
    )(parts)


def steer_kernel(
    group_ref, owners_hbm, grads_hbm, momentum_hbm, renewed_ref, steered_ref,
    owners_ref, grads_ref, momentum_ref, wide_ref, sems,
):
    blocks = COLS // 128
    chunks = COLS // CHUNK

    def fetch(part):
        lanes = pl.ds(part * CHUNK, CHUNK)
        return pltpu.make_async_copy(grads_hbm.at[:, :, lanes], grads_ref.at[part], sems.at[part])

    fetch_owners = pltpu.make_async_copy(owners_hbm, owners_ref, sems.at[chunks])
    fetch_momentum = pltpu.make_async_copy(momentum_hbm, momentum_ref, sems.at[chunks + 1])
    fetch_owners.start()
    fetch_momentum.start()
    for part in range(chunks):
        fetch(part).start()
    steered_ref[OWN:, :] = jnp.zeros((PAD - OWN, COLS), f32)
    fetch_owners.wait()
    owns_one = owners_ref[0] == group_ref[0]
    chosen = 0
    for index in range(1, MATS):
        here = owners_ref[index] == group_ref[0]
        owns_one = jnp.logical_or(owns_one, here)
        chosen = chosen + jnp.where(here, index, 0)
    fetch_momentum.wait()
    for block in range(blocks):
        part, inner = block // (CHUNK // 128), block % (CHUNK // 128)
        if inner == 0:
            fetch(part).wait()
        wide = grads_ref[part, :, :, inner * 128 : (inner + 1) * 128].astype(f32)
        wide_ref[block] = wide.reshape(OWN * MATS, 128)
        gradient = wide_ref[block, pl.ds(chosen, OWN, stride=MATS), :]
        held_state = momentum_ref[pl.ds(block, OWN, stride=blocks), :]
        renewed = jnp.where(owns_one, MOMENTUM_BETA * held_state + gradient, held_state)
        renewed_ref[pl.ds(block, OWN, stride=blocks), :] = renewed
        steered_ref[:OWN, block * 128 : (block + 1) * 128] = gradient + MOMENTUM_BETA * renewed


def in_hbm(value):
    return pltpu.with_memory_space_constraint(value, pltpu.HBM)


def steer(owners, group, grads, momentum):
    chunks = COLS // CHUNK
    return pl.pallas_call(
        steer_kernel,
        in_specs=[pl.BlockSpec(memory_space=pltpu.SMEM)] + [pl.BlockSpec(memory_space=pltpu.HBM)] * 3,
        out_specs=[pl.BlockSpec(memory_space=pltpu.VMEM)] * 2,
        out_shape=[
            jax.ShapeDtypeStruct((OWN * COLS // 128, 128), f32),
            jax.ShapeDtypeStruct((PAD, COLS), f32),
        ],
        scratch_shapes=[
            pltpu.SMEM((MATS,), jnp.int32),
            pltpu.VMEM((chunks, OWN, MATS, CHUNK), bf16),
            pltpu.VMEM((OWN * COLS // 128, 128), f32),
            pltpu.VMEM((COLS // 128, OWN * MATS, 128), f32),
            pltpu.SemaphoreType.DMA((chunks + 2,)),
        ],
        compiler_params=pltpu.CompilerParams(vmem_limit_bytes=32 * 1024 * 1024),
    )(group, in_hbm(owners), in_hbm(grads), in_hbm(momentum))


def exchange(copies, groups):
    return lax.all_to_all(copies, "rep", split_axis=0, concat_axis=0, tiled=True, axis_index_groups=groups)


def deliver(pieces, owners):
    along_y = [[x * NY + y for y in range(NY)] for x in range(NX)]
    along_x = [[x * NY + y for x in range(NX)] for y in range(NY)]
    arrived = lax.all_to_all(pieces, "rep", split_axis=0, concat_axis=0, tiled=True)
    column = exchange(choose(owners, arrived), along_y)
    copies = jnp.broadcast_to(column[None], (NX, *column.shape))
    parts = exchange(copies, along_x)
    rows = assemble(parts.reshape(NX, NY * HALF, MATS, 128))
    return rows.transpose(1, 0, 2)


def shards(grads, momentum, owners):
    group = lax.axis_index("rep").astype(jnp.int32)[None]
    position = lax.axis_index("fsdp").astype(jnp.int32)[None]
    flat = momentum.reshape(OWN * COLS // 128, 128)
    renewed, steered = steer(owners, group, grads.transpose(1, 0, 2), flat)
    whole = lax.all_gather(steered, "fsdp", axis=0, tiled=True)
    pieces = orthogonal_rows(position, in_hbm(whole))
    update = deliver(pieces, owners)
    return (update, renewed.reshape(1, OWN, COLS))


def solution(mesh):
    in_specs = (P(None, "fsdp", None), P("rep", "fsdp", None), P())
    out_specs = (P(None, "fsdp", None), P("rep", "fsdp", None))
    return jax.shard_map(shards, mesh=mesh, in_specs=in_specs, out_specs=out_specs, check_vma=False)
```

```python
import math

import jax
import jax.numpy as jnp
from jax import lax
from jax.experimental import pallas as pl
from jax.experimental.pallas import tpu as pltpu
from jax.sharding import PartitionSpec as P

ROWS = 576
COLS = 2048
MATS = 8
ITERS = 3
N_FSDP = 16
OWN = ROWS // N_FSDP
PAD = 40
TALL = PAD * N_FSDP
NX, NY = 4, 8
N_REP = NX * NY
CHUNK = 512
SHARE = 8
WIDE = COLS // SHARE
SIDES = WIDE // 128
TALL_PIECE = OWN * SIDES

EPSILON = 1e-07
MOMENTUM_BETA = 0.95
QUINTIC_A = 3.4445
QUINTIC_B = -4.775
QUINTIC_C = 2.0315

f32, bf16 = jnp.float32, jnp.bfloat16


def member(group):
    return group // NY * 2 + group % 2


def teams():
    return [[x * NY + y + b for x in range(NX) for b in range(2)] for y in range(0, NY, 2)]


def split(value):
    high = value.astype(bf16)
    low = (value - high.astype(f32)).astype(bf16)
    return high, low


def dot(left, right):
    return jnp.dot(left, right, preferred_element_type=f32)


def dot_nt(left, right):
    return lax.dot_general(left, right, (((1,), (1,)), ((), ())), preferred_element_type=f32)


def product(left, right):
    (lh, ll), (rh, rl) = left, right
    return (dot(lh, rl) + dot(ll, rh)) + dot(lh, rh)


def square(halves):
    high, low = halves
    cross = dot(high, low)
    return (cross + cross.T) + dot(high, high)


def thin_product(rows, halves):
    high, low = halves
    kept = rows.astype(bf16).astype(f32)
    stacked = jnp.concatenate([kept, rows - kept], axis=0).astype(bf16)
    first = dot(stacked, high)
    second = dot(stacked, low)
    return first[:PAD] + (first[PAD:] + second[:PAD])


def orthogonal_kernel(me_ref, s_hbm, u_ref, s_ref, high_ref, low_ref, rows_ref, sems):
    chunks = COLS // CHUNK

    def fetch(part):
        lanes = pl.ds(part * CHUNK, CHUNK)
        return pltpu.make_async_copy(s_hbm.at[:, lanes], s_ref.at[part], sems.at[part])

    for part in range(chunks):
        fetch(part).start()
    gram = None
    cross = None
    for part in range(chunks):
        fetch(part).wait()
        high, low = split(s_ref[part])
        high_ref[part] = high
        low_ref[part] = low
        more_cross, more = dot_nt(high, low), dot_nt(high, high)
        cross = more_cross if part == 0 else cross + more_cross
        gram = more if part == 0 else gram + more
    gram = gram + (cross + cross.T)

    row = lax.broadcasted_iota(jnp.int32, (TALL, TALL), 0)
    col = lax.broadcasted_iota(jnp.int32, (TALL, TALL), 1)
    diagonal = row == col
    total = jnp.sum(jnp.where(diagonal, gram, 0.0), axis=(0, 1), keepdims=True)
    inverse = 1.0 / (jnp.sqrt(total) + EPSILON)
    start = pl.multiple_of(me_ref[0] * PAD, 8)

    def poly(gram, squared):
        return jnp.where(diagonal, QUINTIC_A, 0.0) + QUINTIC_B * gram + QUINTIC_C * squared

    g0 = gram * inverse * inverse
    g0s = split(g0)
    q1s = split(poly(g0, square(g0s)))
    g1 = product(g0s, split(square(q1s)))
    g1s = split(g1)
    q2 = poly(g1, square(g1s))
    q2s = split(q2)
    rows_ref[...] = q2
    mixed = thin_product(rows_ref[pl.ds(start, PAD), :], q1s)

    def by_g2(rows):
        return thin_product(thin_product(thin_product(rows, g1s), q2s), q2s)

    once = by_g2(mixed)
    twice = by_g2(once)
    mixed = QUINTIC_A * mixed + QUINTIC_B * once + QUINTIC_C * twice
    factor = 0.2 * math.sqrt(max(ROWS, COLS))
    for part in range(chunks):
        update = thin_product(mixed, (high_ref[part], low_ref[part])) * inverse * factor
        for inner in range(CHUNK // WIDE):
            lane = inner * WIDE
            sides = [update[:OWN, lane + side * 128 : lane + (side + 1) * 128] for side in range(SIDES)]
            piece = jnp.concatenate(sides, axis=0).astype(bf16)
            for group in range(N_REP):
                if member(group) == part * (CHUNK // WIDE) + inner:
                    u_ref[group] = piece


def orthogonal_rows(position, whole):
    chunks = COLS // CHUNK
    return pl.pallas_call(
        orthogonal_kernel,
        out_shape=jax.ShapeDtypeStruct((N_REP, TALL_PIECE, 128), bf16),
        in_specs=[
            pl.BlockSpec(memory_space=pltpu.SMEM),
            pl.BlockSpec(memory_space=pltpu.HBM),
        ],
        out_specs=pl.BlockSpec(memory_space=pltpu.VMEM),
        scratch_shapes=[
            pltpu.VMEM((chunks, TALL, CHUNK), f32),
            pltpu.VMEM((chunks, TALL, CHUNK), bf16),
            pltpu.VMEM((chunks, TALL, CHUNK), bf16),
            pltpu.VMEM((TALL, TALL), f32),
            pltpu.SemaphoreType.DMA((chunks,)),
        ],
        compiler_params=pltpu.CompilerParams(vmem_limit_bytes=48 * 1024 * 1024),
    )(position, whole)


def choose_kernel(owners_ref, arrived_ref, out_ref, rows_ref):
    for mat in range(MATS):
        rows_ref[pl.ds(mat, TALL_PIECE, stride=MATS), :] = arrived_ref[owners_ref[mat]].astype(f32)
    rows = rows_ref[...].astype(bf16)
    for copy in range(SHARE):
        out_ref[copy] = rows


def choose(owners, arrived):
    return pl.pallas_call(
        choose_kernel,
        out_shape=jax.ShapeDtypeStruct((SHARE, TALL_PIECE * MATS, 128), bf16),
        in_specs=[pl.BlockSpec(memory_space=pltpu.SMEM), pl.BlockSpec(memory_space=pltpu.VMEM)],
        out_specs=pl.BlockSpec(memory_space=pltpu.VMEM),
        scratch_shapes=[pltpu.VMEM((TALL_PIECE * MATS, 128), f32)],
        compiler_params=pltpu.CompilerParams(vmem_limit_bytes=16 * 1024 * 1024),
    )(owners, arrived)


def assemble_kernel(parts_ref, out_hbm, rows_ref, sems):
    half = OWN // 2

    def store(step):
        rows = pl.ds(step * half, half)
        return pltpu.make_async_copy(rows_ref.at[rows], out_hbm.at[rows], sems.at[step])

    for step in range(2):
        for part in range(SHARE):
            for side in range(SIDES):
                lane = part * WIDE + side * 128
                first = side * OWN + step * half
                rows_ref[step * half : (step + 1) * half, :, lane : lane + 128] = parts_ref[part, first : first + half]
        store(step).start()
    for step in range(2):
        store(step).wait()


def assemble(parts):
    return pl.pallas_call(
        assemble_kernel,
        out_shape=pltpu.HBM((OWN, MATS, COLS), bf16),
        in_specs=[pl.BlockSpec(memory_space=pltpu.VMEM)],
        out_specs=pl.BlockSpec(memory_space=pltpu.HBM),
        scratch_shapes=[pltpu.VMEM((OWN, MATS, COLS), bf16), pltpu.SemaphoreType.DMA((2,))],
        compiler_params=pltpu.CompilerParams(vmem_limit_bytes=32 * 1024 * 1024),
    )(parts)


def steer_kernel(
    group_ref, owners_hbm, grads_hbm, momentum_hbm, renewed_ref, steered_ref,
    owners_ref, grads_ref, momentum_ref, wide_ref, sems,
):
    blocks = COLS // 128
    chunks = COLS // CHUNK

    def fetch(part):
        lanes = pl.ds(part * CHUNK, CHUNK)
        return pltpu.make_async_copy(grads_hbm.at[:, :, lanes], grads_ref.at[part], sems.at[part])

    fetch_owners = pltpu.make_async_copy(owners_hbm, owners_ref, sems.at[chunks])
    fetch_momentum = pltpu.make_async_copy(momentum_hbm, momentum_ref, sems.at[chunks + 1])
    fetch_owners.start()
    fetch_momentum.start()
    for part in range(chunks):
        fetch(part).start()
    steered_ref[OWN:, :] = jnp.zeros((PAD - OWN, COLS), f32)
    fetch_owners.wait()
    owns_one = owners_ref[0] == group_ref[0]
    chosen = 0
    for index in range(1, MATS):
        here = owners_ref[index] == group_ref[0]
        owns_one = jnp.logical_or(owns_one, here)
        chosen = chosen + jnp.where(here, index, 0)
    fetch_momentum.wait()
    for block in range(blocks):
        part, inner = block // (CHUNK // 128), block % (CHUNK // 128)
        if inner == 0:
            fetch(part).wait()
        wide = grads_ref[part, :, :, inner * 128 : (inner + 1) * 128].astype(f32)
        wide_ref[block] = wide.reshape(OWN * MATS, 128)
        gradient = wide_ref[block, pl.ds(chosen, OWN, stride=MATS), :]
        held_state = momentum_ref[pl.ds(block, OWN, stride=blocks), :]
        renewed = jnp.where(owns_one, MOMENTUM_BETA * held_state + gradient, held_state)
        renewed_ref[pl.ds(block, OWN, stride=blocks), :] = renewed
        steered_ref[:OWN, block * 128 : (block + 1) * 128] = gradient + MOMENTUM_BETA * renewed


def in_hbm(value):
    return pltpu.with_memory_space_constraint(value, pltpu.HBM)


def steer(owners, group, grads, momentum):
    chunks = COLS // CHUNK
    return pl.pallas_call(
        steer_kernel,
        in_specs=[pl.BlockSpec(memory_space=pltpu.SMEM)] + [pl.BlockSpec(memory_space=pltpu.HBM)] * 3,
        out_specs=[pl.BlockSpec(memory_space=pltpu.VMEM)] * 2,
        out_shape=[
            jax.ShapeDtypeStruct((OWN * COLS // 128, 128), f32),
            jax.ShapeDtypeStruct((PAD, COLS), f32),
        ],
        scratch_shapes=[
            pltpu.SMEM((MATS,), jnp.int32),
            pltpu.VMEM((chunks, OWN, MATS, CHUNK), bf16),
            pltpu.VMEM((OWN * COLS // 128, 128), f32),
            pltpu.VMEM((COLS // 128, OWN * MATS, 128), f32),
            pltpu.SemaphoreType.DMA((chunks + 2,)),
        ],
        compiler_params=pltpu.CompilerParams(vmem_limit_bytes=32 * 1024 * 1024),
    )(group, in_hbm(owners), in_hbm(grads), in_hbm(momentum))


def deliver(pieces, owners):
    arrived = lax.all_to_all(pieces, "rep", split_axis=0, concat_axis=0, tiled=True)
    copies = choose(owners, arrived)
    parts = lax.all_to_all(copies, "rep", split_axis=0, concat_axis=0, tiled=True, axis_index_groups=teams())
    rows = assemble(parts.reshape(SHARE, TALL_PIECE, MATS, 128))
    return rows.transpose(1, 0, 2)


def shards(grads, momentum, owners):
    group = lax.axis_index("rep").astype(jnp.int32)[None]
    position = lax.axis_index("fsdp").astype(jnp.int32)[None]
    flat = momentum.reshape(OWN * COLS // 128, 128)
    renewed, steered = steer(owners, group, grads.transpose(1, 0, 2), flat)
    whole = lax.all_gather(steered, "fsdp", axis=0, tiled=True)
    pieces = orthogonal_rows(position, in_hbm(whole))
    update = deliver(pieces, owners)
    return (update, renewed.reshape(1, OWN, COLS))


def solution(mesh):
    in_specs = (P(None, "fsdp", None), P("rep", "fsdp", None), P())
    out_specs = (P(None, "fsdp", None), P("rep", "fsdp", None))
    return jax.shard_map(shards, mesh=mesh, in_specs=in_specs, out_specs=out_specs, check_vma=False)
```

```python
import math

import jax
import jax.numpy as jnp
from jax import lax
from jax.experimental import pallas as pl
from jax.experimental.pallas import tpu as pltpu
from jax.sharding import PartitionSpec as P

ROWS = 576
COLS = 2048
MATS = 8
ITERS = 3
N_FSDP = 16
OWN = ROWS // N_FSDP
PAD = 40
STEM = 32
TAIL = OWN - STEM
NX, NY = 4, 8
N_REP = NX * NY
CHUNK = 512
SHARE = 8
WIDE = COLS // SHARE
SIDES = WIDE // 128
TALL_PIECE = OWN * SIDES

EPSILON = 1e-07
MOMENTUM_BETA = 0.95
QUINTIC_A = 3.4445
QUINTIC_B = -4.775
QUINTIC_C = 2.0315

f32, bf16 = jnp.float32, jnp.bfloat16


def member(group):
    return group // NY * 2 + group % 2


def teams():
    return [[x * NY + y + b for x in range(NX) for b in range(2)] for y in range(0, NY, 2)]


def split(value):
    high = value.astype(bf16)
    low = (value - high.astype(f32)).astype(bf16)
    return high, low


def dot(left, right):
    return jnp.dot(left, right, preferred_element_type=f32)


def dot_nt(left, right):
    return lax.dot_general(left, right, (((1,), (1,)), ((), ())), preferred_element_type=f32)


def product(left, right):
    (lh, ll), (rh, rl) = left, right
    return (dot(lh, rl) + dot(ll, rh)) + dot(lh, rh)


def square(halves):
    high, low = halves
    cross = dot(high, low)
    return (cross + cross.T) + dot(high, high)


def thin_product(rows, halves):
    high, low = halves
    kept = rows.astype(bf16).astype(f32)
    stacked = jnp.concatenate([kept, rows - kept], axis=0).astype(bf16)
    first = dot(stacked, high)
    second = dot(stacked, low)
    return first[:PAD] + (first[PAD:] + second[:PAD])


def orthogonal_kernel(me_ref, s_hbm, u_ref, stem_ref, tail_ref, high_ref, low_ref, sems):
    chunks = COLS // CHUNK
    blocks = CHUNK // 128

    def fetch(part):
        rows = pl.ds(part * blocks * STEM, blocks * STEM)
        return pltpu.make_async_copy(s_hbm.at[:, rows, :], stem_ref.at[part], sems.at[part])

    tails = pl.ds(COLS // 128 * STEM, COLS // 128 * TAIL)
    fetch_tails = pltpu.make_async_copy(s_hbm.at[:, tails, :], tail_ref, sems.at[chunks])
    fetch_tails.start()
    for part in range(chunks):
        fetch(part).start()
    fetch_tails.wait()
    gram = None
    cross = None
    for part in range(chunks):
        fetch(part).wait()
        columns = []
        for inner in range(blocks):
            stem = stem_ref[part, :, inner * STEM : (inner + 1) * STEM, :].reshape(N_FSDP * STEM, 128)
            first = (part * blocks + inner) * TAIL
            tail = [tail_ref[device, first : first + TAIL, :] for device in range(N_FSDP)]
            columns.append(jnp.concatenate([stem] + tail, axis=0))
        high, low = split(jnp.concatenate(columns, axis=1))
        high_ref[part] = high
        low_ref[part] = low
        more_cross, more = dot_nt(high, low), dot_nt(high, high)
        cross = more_cross if part == 0 else cross + more_cross
        gram = more if part == 0 else gram + more
    gram = gram + (cross + cross.T)

    row = lax.broadcasted_iota(jnp.int32, (ROWS, ROWS), 0)
    col = lax.broadcasted_iota(jnp.int32, (ROWS, ROWS), 1)
    diagonal = row == col
    total = jnp.sum(jnp.where(diagonal, gram, 0.0), axis=(0, 1), keepdims=True)
    inverse = 1.0 / (jnp.sqrt(total) + EPSILON)
    g0 = gram * inverse * inverse
    g0s = split(g0)
    q1s = split(jnp.where(diagonal, QUINTIC_A, 0.0) + QUINTIC_B * g0 + QUINTIC_C * square(g0s))
    g1s = split(product(g0s, split(square(q1s))))

    def by_g1(rows):
        return thin_product(rows, g1s)

    def quintic(rows, once, twice):
        return QUINTIC_A * rows + QUINTIC_B * once + QUINTIC_C * twice

    def by_q2(rows):
        once = by_g1(rows)
        return quintic(rows, once, by_g1(once))

    def by_g2(rows):
        return by_q2(by_q2(by_g1(rows)))

    local = lax.broadcasted_iota(jnp.int32, (PAD, ROWS), 0)
    here = lax.broadcasted_iota(jnp.int32, (PAD, ROWS), 1)
    in_stem = me_ref[0] * STEM + local
    in_tail = N_FSDP * STEM + me_ref[0] * TAIL + local - STEM
    own = jnp.where(local < STEM, in_stem, jnp.where(local < OWN, in_tail, -1))
    unit = jnp.where(own == here, 1.0, 0.0)
    mixed = thin_product(by_q2(unit), q1s)
    once = by_g2(mixed)
    mixed = quintic(mixed, once, by_g2(once))
    factor = 0.2 * math.sqrt(max(ROWS, COLS))
    for part in range(chunks):
        update = thin_product(mixed, (high_ref[part], low_ref[part])) * inverse * factor
        for inner in range(CHUNK // WIDE):
            lane = inner * WIDE
            sides = [update[:OWN, lane + side * 128 : lane + (side + 1) * 128] for side in range(SIDES)]
            piece = jnp.concatenate(sides, axis=0).astype(bf16)
            for group in range(N_REP):
                if member(group) == part * (CHUNK // WIDE) + inner:
                    u_ref[group] = piece


def orthogonal_rows(position, whole):
    chunks = COLS // CHUNK
    return pl.pallas_call(
        orthogonal_kernel,
        out_shape=jax.ShapeDtypeStruct((N_REP, TALL_PIECE, 128), bf16),
        in_specs=[
            pl.BlockSpec(memory_space=pltpu.SMEM),
            pl.BlockSpec(memory_space=pltpu.HBM),
        ],
        out_specs=pl.BlockSpec(memory_space=pltpu.VMEM),
        scratch_shapes=[
            pltpu.VMEM((chunks, N_FSDP, CHUNK // 128 * STEM, 128), f32),
            pltpu.VMEM((N_FSDP, COLS // 128 * TAIL, 128), f32),
            pltpu.VMEM((chunks, ROWS, CHUNK), bf16),
            pltpu.VMEM((chunks, ROWS, CHUNK), bf16),
            pltpu.SemaphoreType.DMA((chunks + 1,)),
        ],
        compiler_params=pltpu.CompilerParams(vmem_limit_bytes=48 * 1024 * 1024),
    )(position, whole)


def choose_kernel(owners_ref, arrived_ref, out_ref, rows_ref):
    for mat in range(MATS):
        rows_ref[pl.ds(mat, TALL_PIECE, stride=MATS), :] = arrived_ref[owners_ref[mat]].astype(f32)
    rows = rows_ref[...].astype(bf16)
    for copy in range(SHARE):
        out_ref[copy] = rows


def choose(owners, arrived):
    return pl.pallas_call(
        choose_kernel,
        out_shape=jax.ShapeDtypeStruct((SHARE, TALL_PIECE * MATS, 128), bf16),
        in_specs=[pl.BlockSpec(memory_space=pltpu.SMEM), pl.BlockSpec(memory_space=pltpu.VMEM)],
        out_specs=pl.BlockSpec(memory_space=pltpu.VMEM),
        scratch_shapes=[pltpu.VMEM((TALL_PIECE * MATS, 128), f32)],
        compiler_params=pltpu.CompilerParams(vmem_limit_bytes=16 * 1024 * 1024),
    )(owners, arrived)


def assemble_kernel(parts_ref, out_hbm, rows_ref, sems):
    half = OWN // 2

    def store(step):
        rows = pl.ds(step * half, half)
        return pltpu.make_async_copy(rows_ref.at[rows], out_hbm.at[rows], sems.at[step])

    for step in range(2):
        for part in range(SHARE):
            for side in range(SIDES):
                lane = part * WIDE + side * 128
                first = side * OWN + step * half
                rows_ref[step * half : (step + 1) * half, :, lane : lane + 128] = parts_ref[part, first : first + half]
        store(step).start()
    for step in range(2):
        store(step).wait()


def assemble(parts):
    return pl.pallas_call(
        assemble_kernel,
        out_shape=pltpu.HBM((OWN, MATS, COLS), bf16),
        in_specs=[pl.BlockSpec(memory_space=pltpu.VMEM)],
        out_specs=pl.BlockSpec(memory_space=pltpu.HBM),
        scratch_shapes=[pltpu.VMEM((OWN, MATS, COLS), bf16), pltpu.SemaphoreType.DMA((2,))],
        compiler_params=pltpu.CompilerParams(vmem_limit_bytes=32 * 1024 * 1024),
    )(parts)


def steer_kernel(
    group_ref, owners_hbm, grads_hbm, momentum_hbm, renewed_ref, steered_ref,
    owners_ref, grads_ref, momentum_ref, wide_ref, sems,
):
    blocks = COLS // 128
    chunks = COLS // CHUNK

    def fetch(part):
        lanes = pl.ds(part * CHUNK, CHUNK)
        return pltpu.make_async_copy(grads_hbm.at[:, :, lanes], grads_ref.at[part], sems.at[part])

    fetch_owners = pltpu.make_async_copy(owners_hbm, owners_ref, sems.at[chunks])
    fetch_momentum = pltpu.make_async_copy(momentum_hbm, momentum_ref, sems.at[chunks + 1])
    fetch_owners.start()
    fetch_momentum.start()
    for part in range(chunks):
        fetch(part).start()
    fetch_owners.wait()
    owns_one = owners_ref[0] == group_ref[0]
    chosen = 0
    for index in range(1, MATS):
        here = owners_ref[index] == group_ref[0]
        owns_one = jnp.logical_or(owns_one, here)
        chosen = chosen + jnp.where(here, index, 0)
    fetch_momentum.wait()
    for block in range(blocks):
        part, inner = block // (CHUNK // 128), block % (CHUNK // 128)
        if inner == 0:
            fetch(part).wait()
        wide = grads_ref[part, :, :, inner * 128 : (inner + 1) * 128].astype(f32)
        wide_ref[block] = wide.reshape(OWN * MATS, 128)
        gradient = wide_ref[block, pl.ds(chosen, OWN, stride=MATS), :]
        held_state = momentum_ref[pl.ds(block, OWN, stride=blocks), :]
        renewed = jnp.where(owns_one, MOMENTUM_BETA * held_state + gradient, held_state)
        renewed_ref[pl.ds(block, OWN, stride=blocks), :] = renewed
        steered = gradient + MOMENTUM_BETA * renewed
        steered_ref[block * STEM : (block + 1) * STEM, :] = steered[:STEM]
        first = blocks * STEM + block * TAIL
        steered_ref[first : first + TAIL, :] = steered[STEM:]


def in_hbm(value):
    return pltpu.with_memory_space_constraint(value, pltpu.HBM)


def steer(owners, group, grads, momentum):
    chunks = COLS // CHUNK
    return pl.pallas_call(
        steer_kernel,
        in_specs=[pl.BlockSpec(memory_space=pltpu.SMEM)] + [pl.BlockSpec(memory_space=pltpu.HBM)] * 3,
        out_specs=[pl.BlockSpec(memory_space=pltpu.VMEM)] * 2,
        out_shape=[
            jax.ShapeDtypeStruct((OWN * COLS // 128, 128), f32),
            jax.ShapeDtypeStruct((OWN * COLS // 128, 128), f32),
        ],
        scratch_shapes=[
            pltpu.SMEM((MATS,), jnp.int32),
            pltpu.VMEM((chunks, OWN, MATS, CHUNK), bf16),
            pltpu.VMEM((OWN * COLS // 128, 128), f32),
            pltpu.VMEM((COLS // 128, OWN * MATS, 128), f32),
            pltpu.SemaphoreType.DMA((chunks + 2,)),
        ],
        compiler_params=pltpu.CompilerParams(vmem_limit_bytes=32 * 1024 * 1024),
    )(group, in_hbm(owners), in_hbm(grads), in_hbm(momentum))


def deliver(pieces, owners):
    arrived = lax.all_to_all(pieces, "rep", split_axis=0, concat_axis=0, tiled=True)
    copies = choose(owners, arrived)
    parts = lax.all_to_all(copies, "rep", split_axis=0, concat_axis=0, tiled=True, axis_index_groups=teams())
    rows = assemble(parts.reshape(SHARE, TALL_PIECE, MATS, 128))
    return rows.transpose(1, 0, 2)


def shards(grads, momentum, owners):
    group = lax.axis_index("rep").astype(jnp.int32)[None]
    position = lax.axis_index("fsdp").astype(jnp.int32)[None]
    flat = momentum.reshape(OWN * COLS // 128, 128)
    renewed, steered = steer(owners, group, grads.transpose(1, 0, 2), flat)
    whole = lax.all_gather(steered, "fsdp")
    pieces = orthogonal_rows(position, in_hbm(whole))
    update = deliver(pieces, owners)
    return (update, renewed.reshape(1, OWN, COLS))


def solution(mesh):
    in_specs = (P(None, "fsdp", None), P("rep", "fsdp", None), P())
    out_specs = (P(None, "fsdp", None), P("rep", "fsdp", None))
    return jax.shard_map(shards, mesh=mesh, in_specs=in_specs, out_specs=out_specs, check_vma=False)
```

```python
import math

import jax
import jax.numpy as jnp
from jax import lax
from jax.experimental import pallas as pl
from jax.experimental.pallas import tpu as pltpu
from jax.sharding import PartitionSpec as P

ROWS = 576
COLS = 2048
MATS = 8
ITERS = 3
N_FSDP = 16
OWN = ROWS // N_FSDP
PAD = 40
SIDE = 256
STEM = 32
TAIL = OWN - STEM
NX, NY = 4, 8
N_REP = NX * NY
CHUNK = 512
SHARE = 8
WIDE = COLS // SHARE
SIDES = WIDE // 128
TALL_PIECE = OWN * SIDES

EPSILON = 1e-07
MOMENTUM_BETA = 0.95
QUINTIC_A = 3.4445
QUINTIC_B = -4.775
QUINTIC_C = 2.0315

f32, bf16 = jnp.float32, jnp.bfloat16


def member(group):
    return group // NY * 2 + group % 2


def teams():
    return [[x * NY + y + b for x in range(NX) for b in range(2)] for y in range(0, NY, 2)]


def split(value):
    high = value.astype(bf16)
    low = (value - high.astype(f32)).astype(bf16)
    return high, low


def dot(left, right):
    return jnp.dot(left, right, preferred_element_type=f32)


def dot_nt(left, right):
    return lax.dot_general(left, right, (((1,), (1,)), ((), ())), preferred_element_type=f32)


def product(left, right):
    (lh, ll), (rh, rl) = left, right
    deep = 2 * SIDE
    ends = jnp.concatenate([lh[:, deep:], ll[:, deep:], lh[:, deep:]], axis=1)
    tops = jnp.concatenate([rl[deep:], rh[deep:], rh[deep:]], axis=0)
    lh, ll, rh, rl = lh[:, :deep], ll[:, :deep], rh[:deep], rl[:deep]
    return ((dot(lh, rl) + dot(ll, rh)) + dot(ends, tops)) + dot(lh, rh)


def mirror(top, middle, bottom):
    first = jnp.concatenate([top, bottom[:, :SIDE].T], axis=1)
    second = jnp.concatenate([top[:, SIDE:].T, middle, bottom[:, SIDE : 2 * SIDE].T], axis=1)
    return jnp.concatenate([first, second, bottom], axis=0)


BLOCKS = ((0, SIDE, 0, 2 * SIDE), (SIDE, 2 * SIDE, SIDE, 2 * SIDE), (2 * SIDE, ROWS, 0, ROWS))


def symmetric_product(left, right):
    (lh, ll), (rh, rl) = left, right
    return mirror(
        *[product((lh[a:b], ll[a:b]), (rh[:, c:d], rl[:, c:d])) for a, b, c, d in BLOCKS]
    )


def square(halves):
    high, low = halves
    cross = dot(high, low)
    return (cross + cross.T) + mirror(*[dot(high[a:b], high[:, c:d]) for a, b, c, d in BLOCKS])


def thin_product(rows, halves):
    high, low = halves
    kept = rows.astype(bf16).astype(f32)
    stacked = jnp.concatenate([kept, rows - kept], axis=0).astype(bf16)
    first = dot(stacked, high)
    second = dot(stacked[:PAD], low)
    return first[:PAD] + (first[PAD:] + second)


def orthogonal_kernel(me_ref, s_hbm, u_ref, stem_ref, tail_ref, high_ref, low_ref, sems):
    chunks = COLS // CHUNK
    blocks = CHUNK // 128

    def fetch(part):
        rows = pl.ds(part * blocks * STEM, blocks * STEM)
        return pltpu.make_async_copy(s_hbm.at[:, rows, :], stem_ref.at[part], sems.at[part])

    tails = pl.ds(COLS // 128 * STEM, COLS // 128 * TAIL)
    fetch_tails = pltpu.make_async_copy(s_hbm.at[:, tails, :], tail_ref, sems.at[chunks])
    fetch_tails.start()
    for part in range(chunks):
        fetch(part).start()
    fetch_tails.wait()
    gram = None
    cross = None
    for part in range(chunks):
        fetch(part).wait()
        columns = []
        for inner in range(blocks):
            stem = stem_ref[part, :, inner * STEM : (inner + 1) * STEM, :].reshape(N_FSDP * STEM, 128)
            first = (part * blocks + inner) * TAIL
            tail = [tail_ref[device, first : first + TAIL, :] for device in range(N_FSDP)]
            columns.append(jnp.concatenate([stem] + tail, axis=0))
        high, low = split(jnp.concatenate(columns, axis=1))
        high_ref[part] = high
        low_ref[part] = low
        more_cross, more = dot_nt(high, low), dot_nt(high, high)
        cross = more_cross if part == 0 else cross + more_cross
        gram = more if part == 0 else gram + more
    gram = gram + (cross + cross.T)

    row = lax.broadcasted_iota(jnp.int32, (ROWS, ROWS), 0)
    col = lax.broadcasted_iota(jnp.int32, (ROWS, ROWS), 1)
    diagonal = row == col
    total = jnp.sum(jnp.where(diagonal, gram, 0.0), axis=(0, 1), keepdims=True)
    inverse = 1.0 / (jnp.sqrt(total) + EPSILON)
    g0 = gram * inverse * inverse
    g0s = split(g0)
    q1s = split(jnp.where(diagonal, QUINTIC_A, 0.0) + QUINTIC_B * g0 + QUINTIC_C * square(g0s))
    g1s = split(symmetric_product(g0s, split(square(q1s))))

    def by_g1(rows):
        return thin_product(rows, g1s)

    def quintic(rows, once, twice):
        return QUINTIC_A * rows + QUINTIC_B * once + QUINTIC_C * twice

    def by_q2(rows):
        once = by_g1(rows)
        return quintic(rows, once, by_g1(once))

    def by_g2(rows):
        return by_q2(by_q2(by_g1(rows)))

    local = lax.broadcasted_iota(jnp.int32, (PAD, ROWS), 0)
    here = lax.broadcasted_iota(jnp.int32, (PAD, ROWS), 1)
    in_stem = me_ref[0] * STEM + local
    in_tail = N_FSDP * STEM + me_ref[0] * TAIL + local - STEM
    own = jnp.where(local < STEM, in_stem, jnp.where(local < OWN, in_tail, -1))
    unit = jnp.where(own == here, 1.0, 0.0)
    mixed = thin_product(by_q2(unit), q1s)
    once = by_g2(mixed)
    mixed = quintic(mixed, once, by_g2(once))
    factor = 0.2 * math.sqrt(max(ROWS, COLS))
    for part in range(chunks):
        update = thin_product(mixed, (high_ref[part], low_ref[part])) * inverse * factor
        for inner in range(CHUNK // WIDE):
            lane = inner * WIDE
            sides = [update[:OWN, lane + side * 128 : lane + (side + 1) * 128] for side in range(SIDES)]
            piece = jnp.concatenate(sides, axis=0).astype(bf16)
            for group in range(N_REP):
                if member(group) == part * (CHUNK // WIDE) + inner:
                    u_ref[group] = piece


def orthogonal_rows(position, whole):
    chunks = COLS // CHUNK
    return pl.pallas_call(
        orthogonal_kernel,
        out_shape=jax.ShapeDtypeStruct((N_REP, TALL_PIECE, 128), bf16),
        in_specs=[
            pl.BlockSpec(memory_space=pltpu.SMEM),
            pl.BlockSpec(memory_space=pltpu.HBM),
        ],
        out_specs=pl.BlockSpec(memory_space=pltpu.VMEM),
        scratch_shapes=[
            pltpu.VMEM((chunks, N_FSDP, CHUNK // 128 * STEM, 128), f32),
            pltpu.VMEM((N_FSDP, COLS // 128 * TAIL, 128), f32),
            pltpu.VMEM((chunks, ROWS, CHUNK), bf16),
            pltpu.VMEM((chunks, ROWS, CHUNK), bf16),
            pltpu.SemaphoreType.DMA((chunks + 1,)),
        ],
        compiler_params=pltpu.CompilerParams(vmem_limit_bytes=48 * 1024 * 1024),
    )(position, whole)


def choose_kernel(owners_ref, arrived_ref, out_ref, rows_ref):
    for mat in range(MATS):
        rows_ref[pl.ds(mat, TALL_PIECE, stride=MATS), :] = arrived_ref[owners_ref[mat]].astype(f32)
    rows = rows_ref[...].astype(bf16)
    for copy in range(SHARE):
        out_ref[copy] = rows


def choose(owners, arrived):
    return pl.pallas_call(
        choose_kernel,
        out_shape=jax.ShapeDtypeStruct((SHARE, TALL_PIECE * MATS, 128), bf16),
        in_specs=[pl.BlockSpec(memory_space=pltpu.SMEM), pl.BlockSpec(memory_space=pltpu.VMEM)],
        out_specs=pl.BlockSpec(memory_space=pltpu.VMEM),
        scratch_shapes=[pltpu.VMEM((TALL_PIECE * MATS, 128), f32)],
        compiler_params=pltpu.CompilerParams(vmem_limit_bytes=16 * 1024 * 1024),
    )(owners, arrived)


def assemble_kernel(parts_ref, out_hbm, rows_ref, sems):
    half = OWN // 2

    def store(step):
        rows = pl.ds(step * half, half)
        return pltpu.make_async_copy(rows_ref.at[rows], out_hbm.at[rows], sems.at[step])

    for step in range(2):
        for part in range(SHARE):
            for side in range(SIDES):
                lane = part * WIDE + side * 128
                first = side * OWN + step * half
                rows_ref[step * half : (step + 1) * half, :, lane : lane + 128] = parts_ref[part, first : first + half]
        store(step).start()
    for step in range(2):
        store(step).wait()


def assemble(parts):
    return pl.pallas_call(
        assemble_kernel,
        out_shape=pltpu.HBM((OWN, MATS, COLS), bf16),
        in_specs=[pl.BlockSpec(memory_space=pltpu.VMEM)],
        out_specs=pl.BlockSpec(memory_space=pltpu.HBM),
        scratch_shapes=[pltpu.VMEM((OWN, MATS, COLS), bf16), pltpu.SemaphoreType.DMA((2,))],
        compiler_params=pltpu.CompilerParams(vmem_limit_bytes=32 * 1024 * 1024),
    )(parts)


def steer_kernel(
    group_ref, owners_hbm, grads_hbm, momentum_hbm, renewed_ref, steered_ref,
    owners_ref, grads_ref, momentum_ref, wide_ref, sems,
):
    blocks = COLS // 128
    chunks = COLS // CHUNK

    def fetch(part):
        lanes = pl.ds(part * CHUNK, CHUNK)
        return pltpu.make_async_copy(grads_hbm.at[:, :, lanes], grads_ref.at[part], sems.at[part])

    fetch_owners = pltpu.make_async_copy(owners_hbm, owners_ref, sems.at[chunks])
    fetch_momentum = pltpu.make_async_copy(momentum_hbm, momentum_ref, sems.at[chunks + 1])
    fetch_owners.start()
    fetch_momentum.start()
    for part in range(chunks):
        fetch(part).start()
    fetch_owners.wait()
    owns_one = owners_ref[0] == group_ref[0]
    chosen = 0
    for index in range(1, MATS):
        here = owners_ref[index] == group_ref[0]
        owns_one = jnp.logical_or(owns_one, here)
        chosen = chosen + jnp.where(here, index, 0)
    fetch_momentum.wait()
    for block in range(blocks):
        part, inner = block // (CHUNK // 128), block % (CHUNK // 128)
        if inner == 0:
            fetch(part).wait()
        wide = grads_ref[part, :, :, inner * 128 : (inner + 1) * 128].astype(f32)
        wide_ref[block] = wide.reshape(OWN * MATS, 128)
        gradient = wide_ref[block, pl.ds(chosen, OWN, stride=MATS), :]
        held_state = momentum_ref[pl.ds(block, OWN, stride=blocks), :]
        renewed = jnp.where(owns_one, MOMENTUM_BETA * held_state + gradient, held_state)
        renewed_ref[pl.ds(block, OWN, stride=blocks), :] = renewed
        steered = gradient + MOMENTUM_BETA * renewed
        steered_ref[block * STEM : (block + 1) * STEM, :] = steered[:STEM]
        first = blocks * STEM + block * TAIL
        steered_ref[first : first + TAIL, :] = steered[STEM:]


def in_hbm(value):
    return pltpu.with_memory_space_constraint(value, pltpu.HBM)


def steer(owners, group, grads, momentum):
    chunks = COLS // CHUNK
    return pl.pallas_call(
        steer_kernel,
        in_specs=[pl.BlockSpec(memory_space=pltpu.SMEM)] + [pl.BlockSpec(memory_space=pltpu.HBM)] * 3,
        out_specs=[pl.BlockSpec(memory_space=pltpu.VMEM)] * 2,
        out_shape=[
            jax.ShapeDtypeStruct((OWN * COLS // 128, 128), f32),
            jax.ShapeDtypeStruct((OWN * COLS // 128, 128), f32),
        ],
        scratch_shapes=[
            pltpu.SMEM((MATS,), jnp.int32),
            pltpu.VMEM((chunks, OWN, MATS, CHUNK), bf16),
            pltpu.VMEM((OWN * COLS // 128, 128), f32),
            pltpu.VMEM((COLS // 128, OWN * MATS, 128), f32),
            pltpu.SemaphoreType.DMA((chunks + 2,)),
        ],
        compiler_params=pltpu.CompilerParams(vmem_limit_bytes=32 * 1024 * 1024),
    )(group, in_hbm(owners), in_hbm(grads), in_hbm(momentum))


def deliver(pieces, owners):
    arrived = lax.all_to_all(pieces, "rep", split_axis=0, concat_axis=0, tiled=True)
    copies = choose(owners, arrived)
    parts = lax.all_to_all(copies, "rep", split_axis=0, concat_axis=0, tiled=True, axis_index_groups=teams())
    rows = assemble(parts.reshape(SHARE, TALL_PIECE, MATS, 128))
    return rows.transpose(1, 0, 2)


def shards(grads, momentum, owners):
    group = lax.axis_index("rep").astype(jnp.int32)[None]
    position = lax.axis_index("fsdp").astype(jnp.int32)[None]
    flat = momentum.reshape(OWN * COLS // 128, 128)
    renewed, steered = steer(owners, group, grads.transpose(1, 0, 2), flat)
    whole = lax.all_gather(steered, "fsdp")
    pieces = orthogonal_rows(position, in_hbm(whole))
    update = deliver(pieces, owners)
    return (update, renewed.reshape(1, OWN, COLS))


def solution(mesh):
    in_specs = (P(None, "fsdp", None), P("rep", "fsdp", None), P())
    out_specs = (P(None, "fsdp", None), P("rep", "fsdp", None))
    return jax.shard_map(shards, mesh=mesh, in_specs=in_specs, out_specs=out_specs, check_vma=False)
```

```python
import math

import jax
import jax.numpy as jnp
from jax import lax
from jax.experimental import pallas as pl
from jax.experimental.pallas import tpu as pltpu
from jax.sharding import PartitionSpec as P

ROWS = 576
COLS = 2048
MATS = 8
ITERS = 3
N_FSDP = 16
OWN = ROWS // N_FSDP
PAD = 40
SIDE = 256
STEM = 32
TAIL = OWN - STEM
NX, NY = 4, 8
N_REP = NX * NY
CHUNK = 512
SHARE = 8
WIDE = COLS // SHARE
SIDES = WIDE // 128
TALL_PIECE = OWN * SIDES

EPSILON = 1e-07
MOMENTUM_BETA = 0.95
QUINTIC_A = 3.4445
QUINTIC_B = -4.775
QUINTIC_C = 2.0315

f32, bf16 = jnp.float32, jnp.bfloat16


def member(group):
    return group // NY * 2 + group % 2


def teams():
    return [[x * NY + y + b for x in range(NX) for b in range(2)] for y in range(0, NY, 2)]


def split(value):
    high = value.astype(bf16)
    low = (value - high.astype(f32)).astype(bf16)
    return high, low


def dot(left, right):
    return jnp.dot(left, right, preferred_element_type=f32)


def dot_nt(left, right):
    return lax.dot_general(left, right, (((1,), (1,)), ((), ())), preferred_element_type=f32)


def product(left, right):
    (lh, ll), (rh, rl) = left, right
    deep = 2 * SIDE
    ends = jnp.concatenate([lh[:, deep:], ll[:, deep:], lh[:, deep:]], axis=1)
    tops = jnp.concatenate([rl[deep:], rh[deep:], rh[deep:]], axis=0)
    lh, ll, rh, rl = lh[:, :deep], ll[:, :deep], rh[:deep], rl[:deep]
    return ((dot(lh, rl) + dot(ll, rh)) + dot(ends, tops)) + dot(lh, rh)


def mirror(top, middle, bottom):
    first = jnp.concatenate([top, bottom[:, :SIDE].T], axis=1)
    second = jnp.concatenate([top[:, SIDE:].T, middle, bottom[:, SIDE : 2 * SIDE].T], axis=1)
    return jnp.concatenate([first, second, bottom], axis=0)


BLOCKS = ((0, SIDE, 0, 2 * SIDE), (SIDE, 2 * SIDE, SIDE, 2 * SIDE), (2 * SIDE, ROWS, 0, ROWS))


def symmetric_product(left, right):
    (lh, ll), (rh, rl) = left, right
    return mirror(
        *[product((lh[a:b], ll[a:b]), (rh[:, c:d], rl[:, c:d])) for a, b, c, d in BLOCKS]
    )


def square(halves):
    high, low = halves
    cross = dot(high, low)
    return (cross + cross.T) + mirror(*[dot(high[a:b], high[:, c:d]) for a, b, c, d in BLOCKS])


def thin_product(rows, halves):
    high, low = halves
    kept = rows.astype(bf16).astype(f32)
    stacked = jnp.concatenate([kept, rows - kept], axis=0).astype(bf16)
    first = dot(stacked, high)
    second = dot(stacked[:PAD], low)
    return first[:PAD] + (first[PAD:] + second)


def orthogonal_kernel(me_ref, s_hbm, greeting_hbm, meeting_hbm, u_ref, stem_ref, tail_ref, high_ref, low_ref, sems):
    chunks = COLS // CHUNK
    blocks = CHUNK // 128

    def fetch(part):
        rows = pl.ds(part * blocks * STEM, blocks * STEM)
        return pltpu.make_async_copy(s_hbm.at[:, rows, :], stem_ref.at[part], sems.at[part])

    tails = pl.ds(COLS // 128 * STEM, COLS // 128 * TAIL)
    fetch_tails = pltpu.make_async_copy(s_hbm.at[:, tails, :], tail_ref, sems.at[chunks])
    fetch_tails.start()
    for part in range(chunks):
        fetch(part).start()
    fetch_tails.wait()
    gram = None
    cross = None
    for part in range(chunks):
        fetch(part).wait()
        columns = []
        for inner in range(blocks):
            stem = stem_ref[part, :, inner * STEM : (inner + 1) * STEM, :].reshape(N_FSDP * STEM, 128)
            first = (part * blocks + inner) * TAIL
            tail = [tail_ref[device, first : first + TAIL, :] for device in range(N_FSDP)]
            columns.append(jnp.concatenate([stem] + tail, axis=0))
        high, low = split(jnp.concatenate(columns, axis=1))
        high_ref[part] = high
        low_ref[part] = low
        more_cross, more = dot_nt(high, low), dot_nt(high, high)
        cross = more_cross if part == 0 else cross + more_cross
        gram = more if part == 0 else gram + more
    gram = gram + (cross + cross.T)

    row = lax.broadcasted_iota(jnp.int32, (ROWS, ROWS), 0)
    col = lax.broadcasted_iota(jnp.int32, (ROWS, ROWS), 1)
    diagonal = row == col
    total = jnp.sum(jnp.where(diagonal, gram, 0.0), axis=(0, 1), keepdims=True)
    inverse = 1.0 / (jnp.sqrt(total) + EPSILON)
    g0 = gram * inverse * inverse
    g0s = split(g0)
    q1s = split(jnp.where(diagonal, QUINTIC_A, 0.0) + QUINTIC_B * g0 + QUINTIC_C * square(g0s))
    g1s = split(symmetric_product(g0s, split(square(q1s))))

    def by_g1(rows):
        return thin_product(rows, g1s)

    def quintic(rows, once, twice):
        return QUINTIC_A * rows + QUINTIC_B * once + QUINTIC_C * twice

    def by_q2(rows):
        once = by_g1(rows)
        return quintic(rows, once, by_g1(once))

    def by_g2(rows):
        return by_q2(by_q2(by_g1(rows)))

    local = lax.broadcasted_iota(jnp.int32, (PAD, ROWS), 0)
    here = lax.broadcasted_iota(jnp.int32, (PAD, ROWS), 1)
    in_stem = me_ref[0] * STEM + local
    in_tail = N_FSDP * STEM + me_ref[0] * TAIL + local - STEM
    own = jnp.where(local < STEM, in_stem, jnp.where(local < OWN, in_tail, -1))
    unit = jnp.where(own == here, 1.0, 0.0)
    mixed = thin_product(by_q2(unit), q1s)
    once = by_g2(mixed)
    mixed = quintic(mixed, once, by_g2(once))
    factor = 0.2 * math.sqrt(max(ROWS, COLS))
    for part in range(chunks):
        update = thin_product(mixed, (high_ref[part], low_ref[part])) * inverse * factor
        for inner in range(CHUNK // WIDE):
            lane = inner * WIDE
            sides = [update[:OWN, lane + side * 128 : lane + (side + 1) * 128] for side in range(SIDES)]
            piece = jnp.concatenate(sides, axis=0).astype(bf16)
            for group in range(N_REP):
                if member(group) == part * (CHUNK // WIDE) + inner:
                    u_ref[group] = piece


def orthogonal_rows(position, whole, greeting, meeting):
    chunks = COLS // CHUNK
    return pl.pallas_call(
        orthogonal_kernel,
        out_shape=jax.ShapeDtypeStruct((N_REP, TALL_PIECE, 128), bf16),
        in_specs=[
            pl.BlockSpec(memory_space=pltpu.SMEM),
            pl.BlockSpec(memory_space=pltpu.HBM),
            pl.BlockSpec(memory_space=pl.ANY),
            pl.BlockSpec(memory_space=pl.ANY),
        ],
        out_specs=pl.BlockSpec(memory_space=pltpu.VMEM),
        scratch_shapes=[
            pltpu.VMEM((chunks, N_FSDP, CHUNK // 128 * STEM, 128), f32),
            pltpu.VMEM((N_FSDP, COLS // 128 * TAIL, 128), f32),
            pltpu.VMEM((chunks, ROWS, CHUNK), bf16),
            pltpu.VMEM((chunks, ROWS, CHUNK), bf16),
            pltpu.SemaphoreType.DMA((chunks + 1,)),
        ],
        compiler_params=pltpu.CompilerParams(vmem_limit_bytes=48 * 1024 * 1024),
    )(position, whole, greeting, meeting)


def choose_kernel(owners_ref, arrived_ref, out_ref, rows_ref):
    for mat in range(MATS):
        rows_ref[pl.ds(mat, TALL_PIECE, stride=MATS), :] = arrived_ref[owners_ref[mat]].astype(f32)
    rows = rows_ref[...].astype(bf16)
    for copy in range(SHARE):
        out_ref[copy] = rows


def choose(owners, arrived):
    return pl.pallas_call(
        choose_kernel,
        out_shape=jax.ShapeDtypeStruct((SHARE, TALL_PIECE * MATS, 128), bf16),
        in_specs=[pl.BlockSpec(memory_space=pltpu.SMEM), pl.BlockSpec(memory_space=pltpu.VMEM)],
        out_specs=pl.BlockSpec(memory_space=pltpu.VMEM),
        scratch_shapes=[pltpu.VMEM((TALL_PIECE * MATS, 128), f32)],
        compiler_params=pltpu.CompilerParams(vmem_limit_bytes=16 * 1024 * 1024),
    )(owners, arrived)


def assemble_kernel(parts_ref, out_hbm, rows_ref, sems):
    half = OWN // 2

    def store(step):
        rows = pl.ds(step * half, half)
        return pltpu.make_async_copy(rows_ref.at[rows], out_hbm.at[rows], sems.at[step])

    for step in range(2):
        for part in range(SHARE):
            for side in range(SIDES):
                lane = part * WIDE + side * 128
                first = side * OWN + step * half
                rows_ref[step * half : (step + 1) * half, :, lane : lane + 128] = parts_ref[part, first : first + half]
        store(step).start()
    for step in range(2):
        store(step).wait()


def assemble(parts):
    return pl.pallas_call(
        assemble_kernel,
        out_shape=pltpu.HBM((OWN, MATS, COLS), bf16),
        in_specs=[pl.BlockSpec(memory_space=pltpu.VMEM)],
        out_specs=pl.BlockSpec(memory_space=pltpu.HBM),
        scratch_shapes=[pltpu.VMEM((OWN, MATS, COLS), bf16), pltpu.SemaphoreType.DMA((2,))],
        compiler_params=pltpu.CompilerParams(vmem_limit_bytes=32 * 1024 * 1024),
    )(parts)


def steer_kernel(
    group_ref, owners_hbm, grads_hbm, momentum_hbm, renewed_ref, steered_ref,
    owners_ref, grads_ref, momentum_ref, wide_ref, sems,
):
    blocks = COLS // 128
    chunks = COLS // CHUNK

    def fetch(part):
        lanes = pl.ds(part * CHUNK, CHUNK)
        return pltpu.make_async_copy(grads_hbm.at[:, :, lanes], grads_ref.at[part], sems.at[part])

    fetch_owners = pltpu.make_async_copy(owners_hbm, owners_ref, sems.at[chunks])
    fetch_momentum = pltpu.make_async_copy(momentum_hbm, momentum_ref, sems.at[chunks + 1])
    fetch_owners.start()
    fetch_momentum.start()
    for part in range(chunks):
        fetch(part).start()
    fetch_owners.wait()
    owns_one = owners_ref[0] == group_ref[0]
    chosen = 0
    for index in range(1, MATS):
        here = owners_ref[index] == group_ref[0]
        owns_one = jnp.logical_or(owns_one, here)
        chosen = chosen + jnp.where(here, index, 0)
    fetch_momentum.wait()
    for block in range(blocks):
        part, inner = block // (CHUNK // 128), block % (CHUNK // 128)
        if inner == 0:
            fetch(part).wait()
        wide = grads_ref[part, :, :, inner * 128 : (inner + 1) * 128].astype(f32)
        wide_ref[block] = wide.reshape(OWN * MATS, 128)
        gradient = wide_ref[block, pl.ds(chosen, OWN, stride=MATS), :]
        held_state = momentum_ref[pl.ds(block, OWN, stride=blocks), :]
        renewed = jnp.where(owns_one, MOMENTUM_BETA * held_state + gradient, held_state)
        renewed_ref[pl.ds(block, OWN, stride=blocks), :] = renewed
        steered = gradient + MOMENTUM_BETA * renewed
        steered_ref[block * STEM : (block + 1) * STEM, :] = steered[:STEM]
        first = blocks * STEM + block * TAIL
        steered_ref[first : first + TAIL, :] = steered[STEM:]


def in_hbm(value):
    return pltpu.with_memory_space_constraint(value, pltpu.HBM)


def steer(owners, group, grads, momentum):
    chunks = COLS // CHUNK
    return pl.pallas_call(
        steer_kernel,
        in_specs=[pl.BlockSpec(memory_space=pltpu.SMEM)] + [pl.BlockSpec(memory_space=pltpu.HBM)] * 3,
        out_specs=[pl.BlockSpec(memory_space=pltpu.VMEM)] * 2,
        out_shape=[
            jax.ShapeDtypeStruct((OWN * COLS // 128, 128), f32),
            jax.ShapeDtypeStruct((OWN * COLS // 128, 128), f32),
        ],
        scratch_shapes=[
            pltpu.SMEM((MATS,), jnp.int32),
            pltpu.VMEM((chunks, OWN, MATS, CHUNK), bf16),
            pltpu.VMEM((OWN * COLS // 128, 128), f32),
            pltpu.VMEM((COLS // 128, OWN * MATS, 128), f32),
            pltpu.SemaphoreType.DMA((chunks + 2,)),
        ],
        compiler_params=pltpu.CompilerParams(vmem_limit_bytes=32 * 1024 * 1024),
    )(group, in_hbm(owners), in_hbm(grads), in_hbm(momentum))


def deliver(pieces, owners):
    arrived = lax.all_to_all(pieces, "rep", split_axis=0, concat_axis=0, tiled=True)
    copies = choose(owners, arrived)
    parts = lax.all_to_all(copies, "rep", split_axis=0, concat_axis=0, tiled=True, axis_index_groups=teams())
    rows = assemble(parts.reshape(SHARE, TALL_PIECE, MATS, 128))
    return rows.transpose(1, 0, 2)


def shards(grads, momentum, owners):
    group = lax.axis_index("rep").astype(jnp.int32)[None]
    position = lax.axis_index("fsdp").astype(jnp.int32)[None]
    flat = momentum.reshape(OWN * COLS // 128, 128)
    renewed, steered = steer(owners, group, grads.transpose(1, 0, 2), flat)
    whole = lax.all_gather(steered, "fsdp")
    greeting = lax.all_to_all(renewed[: N_REP * 8].reshape(N_REP, 8, 128), "rep", split_axis=0, concat_axis=0, tiled=True)
    meeting = lax.all_to_all(
        renewed[: SHARE * 8].reshape(SHARE, 8, 128),
        "rep",
        split_axis=0,
        concat_axis=0,
        tiled=True,
        axis_index_groups=teams(),
    )
    pieces = orthogonal_rows(position, in_hbm(whole), greeting, meeting)
    update = deliver(pieces, owners)
    return (update, renewed.reshape(1, OWN, COLS))


def solution(mesh):
    in_specs = (P(None, "fsdp", None), P("rep", "fsdp", None), P())
    out_specs = (P(None, "fsdp", None), P("rep", "fsdp", None))
    return jax.shard_map(shards, mesh=mesh, in_specs=in_specs, out_specs=out_specs, check_vma=False)
```

```python
import math

import jax
import jax.numpy as jnp
from jax import lax
from jax.experimental import pallas as pl
from jax.experimental.pallas import tpu as pltpu
from jax.sharding import PartitionSpec as P

ROWS = 576
COLS = 2048
MATS = 8
ITERS = 3
N_FSDP = 16
OWN = ROWS // N_FSDP
PAD = 40
SIDE = 256
STEM = 32
TAIL = OWN - STEM
NX, NY = 4, 8
N_REP = NX * NY
CHUNK = 512
SHARE = 8
WIDE = COLS // SHARE
SIDES = WIDE // 128
TALL_PIECE = OWN * SIDES

EPSILON = 1e-07
MOMENTUM_BETA = 0.95
QUINTIC_A = 3.4445
QUINTIC_B = -4.775
QUINTIC_C = 2.0315

f32, bf16 = jnp.float32, jnp.bfloat16


def member(group):
    return group // NY * 2 + group % 2


def teams():
    return [[x * NY + y + b for x in range(NX) for b in range(2)] for y in range(0, NY, 2)]


def split(value):
    high = value.astype(bf16)
    low = (value - high.astype(f32)).astype(bf16)
    return high, low


def dot(left, right):
    return jnp.dot(left, right, preferred_element_type=f32)


def dot_nt(left, right):
    return lax.dot_general(left, right, (((1,), (1,)), ((), ())), preferred_element_type=f32)


def product(left, right):
    (lh, ll), (rh, rl) = left, right
    deep = 2 * SIDE
    ends = jnp.concatenate([lh[:, deep:], ll[:, deep:], lh[:, deep:]], axis=1)
    tops = jnp.concatenate([rl[deep:], rh[deep:], rh[deep:]], axis=0)
    lh, ll, rh, rl = lh[:, :deep], ll[:, :deep], rh[:deep], rl[:deep]
    return ((dot(lh, rl) + dot(ll, rh)) + dot(ends, tops)) + dot(lh, rh)


def mirror(top, middle, bottom):
    first = jnp.concatenate([top, bottom[:, :SIDE].T], axis=1)
    second = jnp.concatenate([top[:, SIDE:].T, middle, bottom[:, SIDE : 2 * SIDE].T], axis=1)
    return jnp.concatenate([first, second, bottom], axis=0)


BLOCKS = ((0, SIDE, 0, 2 * SIDE), (SIDE, 2 * SIDE, SIDE, 2 * SIDE), (2 * SIDE, ROWS, 0, ROWS))


def symmetric_product(left, right):
    (lh, ll), (rh, rl) = left, right
    return mirror(
        *[product((lh[a:b], ll[a:b]), (rh[:, c:d], rl[:, c:d])) for a, b, c, d in BLOCKS]
    )


def square(halves):
    high, low = halves
    cross = dot(high, low)
    return (cross + cross.T) + mirror(*[dot(high[a:b], high[:, c:d]) for a, b, c, d in BLOCKS])


def thin_product(rows, halves):
    high, low = halves
    kept = rows.astype(bf16).astype(f32)
    stacked = jnp.concatenate([kept, rows - kept], axis=0).astype(bf16)
    first = dot(stacked, high)
    second = dot(stacked[:PAD], low)
    return first[:PAD] + (first[PAD:] + second)


def orthogonal_kernel(me_ref, s_hbm, u_ref, stem_ref, tail_ref, high_ref, low_ref, sems):
    chunks = COLS // CHUNK
    blocks = CHUNK // 128

    def fetch(part):
        rows = pl.ds(part * blocks * STEM, blocks * STEM)
        return pltpu.make_async_copy(s_hbm.at[:, rows, :], stem_ref.at[part], sems.at[part])

    tails = pl.ds(COLS // 128 * STEM, COLS // 128 * TAIL)
    fetch_tails = pltpu.make_async_copy(s_hbm.at[:, tails, :], tail_ref, sems.at[chunks])
    fetch_tails.start()
    for part in range(chunks):
        fetch(part).start()
    fetch_tails.wait()
    gram = None
    cross = None
    for part in range(chunks):
        fetch(part).wait()
        columns = []
        for inner in range(blocks):
            stem = stem_ref[part, :, inner * STEM : (inner + 1) * STEM, :].reshape(N_FSDP * STEM, 128)
            first = (part * blocks + inner) * TAIL
            tail = [tail_ref[device, first : first + TAIL, :] for device in range(N_FSDP)]
            columns.append(jnp.concatenate([stem] + tail, axis=0))
        high, low = split(jnp.concatenate(columns, axis=1))
        high_ref[part] = high
        low_ref[part] = low
        more_cross, more = dot_nt(high, low), dot_nt(high, high)
        cross = more_cross if part == 0 else cross + more_cross
        gram = more if part == 0 else gram + more
    gram = gram + (cross + cross.T)

    row = lax.broadcasted_iota(jnp.int32, (ROWS, ROWS), 0)
    col = lax.broadcasted_iota(jnp.int32, (ROWS, ROWS), 1)
    diagonal = row == col
    total = jnp.sum(jnp.where(diagonal, gram, 0.0), axis=(0, 1), keepdims=True)
    inverse = 1.0 / (jnp.sqrt(total) + EPSILON)
    g0 = gram * inverse * inverse
    g0s = split(g0)
    q1s = split(jnp.where(diagonal, QUINTIC_A, 0.0) + QUINTIC_B * g0 + QUINTIC_C * square(g0s))
    g1s = split(symmetric_product(g0s, split(square(q1s))))

    def by_g1(rows):
        return thin_product(rows, g1s)

    def quintic(rows, once, twice):
        return QUINTIC_A * rows + QUINTIC_B * once + QUINTIC_C * twice

    def by_q2(rows):
        once = by_g1(rows)
        return quintic(rows, once, by_g1(once))

    def by_g2(rows):
        return by_q2(by_q2(by_g1(rows)))

    local = lax.broadcasted_iota(jnp.int32, (PAD, ROWS), 0)
    here = lax.broadcasted_iota(jnp.int32, (PAD, ROWS), 1)
    in_stem = me_ref[0] * STEM + local
    in_tail = N_FSDP * STEM + me_ref[0] * TAIL + local - STEM
    own = jnp.where(local < STEM, in_stem, jnp.where(local < OWN, in_tail, -1))
    unit = jnp.where(own == here, 1.0, 0.0)
    mixed = thin_product(by_q2(unit), q1s)
    once = by_g2(mixed)
    mixed = quintic(mixed, once, by_g2(once))
    factor = 0.2 * math.sqrt(max(ROWS, COLS))
    for part in range(chunks):
        update = thin_product(mixed, (high_ref[part], low_ref[part])) * inverse * factor
        for inner in range(CHUNK // WIDE):
            lane = inner * WIDE
            sides = [update[:OWN, lane + side * 128 : lane + (side + 1) * 128] for side in range(SIDES)]
            piece = jnp.concatenate(sides, axis=0).astype(bf16)
            for group in range(N_REP):
                if member(group) == part * (CHUNK // WIDE) + inner:
                    u_ref[group] = piece


def orthogonal_rows(position, whole):
    chunks = COLS // CHUNK
    return pl.pallas_call(
        orthogonal_kernel,
        out_shape=jax.ShapeDtypeStruct((N_REP, TALL_PIECE, 128), bf16),
        in_specs=[
            pl.BlockSpec(memory_space=pltpu.SMEM),
            pl.BlockSpec(memory_space=pltpu.HBM),
        ],
        out_specs=pl.BlockSpec(memory_space=pltpu.VMEM),
        scratch_shapes=[
            pltpu.VMEM((chunks, N_FSDP, CHUNK // 128 * STEM, 128), f32),
            pltpu.VMEM((N_FSDP, COLS // 128 * TAIL, 128), f32),
            pltpu.VMEM((chunks, ROWS, CHUNK), bf16),
            pltpu.VMEM((chunks, ROWS, CHUNK), bf16),
            pltpu.SemaphoreType.DMA((chunks + 1,)),
        ],
        compiler_params=pltpu.CompilerParams(vmem_limit_bytes=48 * 1024 * 1024),
    )(position, whole)


def choose_kernel(owners_ref, arrived_ref, out_ref, rows_ref):
    for mat in range(MATS):
        rows_ref[pl.ds(mat, TALL_PIECE, stride=MATS), :] = arrived_ref[owners_ref[mat]].astype(f32)
    rows = rows_ref[...].astype(bf16)
    for copy in range(SHARE):
        out_ref[copy] = rows


def choose(owners, arrived):
    return pl.pallas_call(
        choose_kernel,
        out_shape=jax.ShapeDtypeStruct((SHARE, TALL_PIECE * MATS, 128), bf16),
        in_specs=[pl.BlockSpec(memory_space=pltpu.SMEM), pl.BlockSpec(memory_space=pltpu.VMEM)],
        out_specs=pl.BlockSpec(memory_space=pltpu.VMEM),
        scratch_shapes=[pltpu.VMEM((TALL_PIECE * MATS, 128), f32)],
        compiler_params=pltpu.CompilerParams(vmem_limit_bytes=16 * 1024 * 1024),
    )(owners, arrived)


def assemble_kernel(parts_ref, out_hbm, rows_ref, sems):
    half = OWN // 2

    def store(step):
        rows = pl.ds(step * half, half)
        return pltpu.make_async_copy(rows_ref.at[rows], out_hbm.at[rows], sems.at[step])

    for step in range(2):
        for part in range(SHARE):
            for side in range(SIDES):
                lane = part * WIDE + side * 128
                first = side * OWN + step * half
                rows_ref[step * half : (step + 1) * half, :, lane : lane + 128] = parts_ref[part, first : first + half]
        store(step).start()
    for step in range(2):
        store(step).wait()


def assemble(parts):
    return pl.pallas_call(
        assemble_kernel,
        out_shape=pltpu.HBM((OWN, MATS, COLS), bf16),
        in_specs=[pl.BlockSpec(memory_space=pltpu.VMEM)],
        out_specs=pl.BlockSpec(memory_space=pltpu.HBM),
        scratch_shapes=[pltpu.VMEM((OWN, MATS, COLS), bf16), pltpu.SemaphoreType.DMA((2,))],
        compiler_params=pltpu.CompilerParams(vmem_limit_bytes=32 * 1024 * 1024),
    )(parts)


def steer_kernel(
    group_ref, owners_hbm, grads_hbm, momentum_hbm, renewed_ref, steered_ref,
    owners_ref, grads_ref, momentum_ref, wide_ref, fresh_ref, sems,
):
    blocks = COLS // 128
    chunks = COLS // CHUNK

    def fetch(part):
        lanes = pl.ds(part * CHUNK, CHUNK)
        return pltpu.make_async_copy(grads_hbm.at[:, :, lanes], grads_ref.at[part], sems.at[part])

    fetch_owners = pltpu.make_async_copy(owners_hbm, owners_ref, sems.at[chunks])
    held_rows = pl.ds(0, OWN * blocks)
    fetch_momentum = pltpu.make_async_copy(momentum_hbm, momentum_ref.at[held_rows], sems.at[chunks + 1])
    fetch_owners.start()
    fetch_momentum.start()
    for part in range(chunks):
        fetch(part).start()
    fetch_owners.wait()
    owns_one = owners_ref[0] == group_ref[0]
    chosen = 0
    for index in range(1, MATS):
        here = owners_ref[index] == group_ref[0]
        owns_one = jnp.logical_or(owns_one, here)
        chosen = chosen + jnp.where(here, index, 0)
    fetch_momentum.wait()
    for block in range(blocks):
        part, inner = block // (CHUNK // 128), block % (CHUNK // 128)
        if inner == 0:
            fetch(part).wait()
        wide = grads_ref[part, :, :, inner * 128 : (inner + 1) * 128].astype(f32)
        wide_ref[block, : OWN * MATS, :] = wide.reshape(OWN * MATS, 128)
        gradient = wide_ref[block, pl.ds(chosen, PAD, stride=MATS), :]
        held_state = momentum_ref[pl.ds(block, PAD, stride=blocks), :]
        renewed = jnp.where(owns_one, MOMENTUM_BETA * held_state + gradient, held_state)
        fresh_ref[pl.ds(block, PAD, stride=blocks), :] = renewed
        steered = gradient + MOMENTUM_BETA * renewed
        steered_ref[block * STEM : (block + 1) * STEM, :] = steered[:STEM]
        first = blocks * STEM + block * TAIL
        steered_ref[first : first + TAIL, :] = steered[STEM:OWN]
    renewed_ref[...] = fresh_ref[: OWN * blocks, :]


def in_hbm(value):
    return pltpu.with_memory_space_constraint(value, pltpu.HBM)


def steer(owners, group, grads, momentum):
    chunks = COLS // CHUNK
    return pl.pallas_call(
        steer_kernel,
        in_specs=[pl.BlockSpec(memory_space=pltpu.SMEM)] + [pl.BlockSpec(memory_space=pltpu.HBM)] * 3,
        out_specs=[pl.BlockSpec(memory_space=pltpu.VMEM)] * 2,
        out_shape=[
            jax.ShapeDtypeStruct((OWN * COLS // 128, 128), f32),
            jax.ShapeDtypeStruct((OWN * COLS // 128, 128), f32),
        ],
        scratch_shapes=[
            pltpu.SMEM((MATS,), jnp.int32),
            pltpu.VMEM((chunks, OWN, MATS, CHUNK), bf16),
            pltpu.VMEM((PAD * COLS // 128, 128), f32),
            pltpu.VMEM((COLS // 128, PAD * MATS, 128), f32),
            pltpu.VMEM((PAD * COLS // 128, 128), f32),
            pltpu.SemaphoreType.DMA((chunks + 2,)),
        ],
        compiler_params=pltpu.CompilerParams(vmem_limit_bytes=32 * 1024 * 1024),
    )(group, in_hbm(owners), in_hbm(grads), in_hbm(momentum))


def deliver(pieces, owners):
    arrived = lax.all_to_all(pieces, "rep", split_axis=0, concat_axis=0, tiled=True)
    copies = choose(owners, arrived)
    parts = lax.all_to_all(copies, "rep", split_axis=0, concat_axis=0, tiled=True, axis_index_groups=teams())
    rows = assemble(parts.reshape(SHARE, TALL_PIECE, MATS, 128))
    return rows.transpose(1, 0, 2)


def shards(grads, momentum, owners):
    group = lax.axis_index("rep").astype(jnp.int32)[None]
    position = lax.axis_index("fsdp").astype(jnp.int32)[None]
    flat = momentum.reshape(OWN * COLS // 128, 128)
    renewed, steered = steer(owners, group, grads.transpose(1, 0, 2), flat)
    whole = lax.all_gather(steered, "fsdp")
    pieces = orthogonal_rows(position, in_hbm(whole))
    update = deliver(pieces, owners)
    return (update, renewed.reshape(1, OWN, COLS))


def solution(mesh):
    in_specs = (P(None, "fsdp", None), P("rep", "fsdp", None), P())
    out_specs = (P(None, "fsdp", None), P("rep", "fsdp", None))
    return jax.shard_map(shards, mesh=mesh, in_specs=in_specs, out_specs=out_specs, check_vma=False)
```

```python
import math

import jax
import jax.numpy as jnp
from jax import lax
from jax.experimental import pallas as pl
from jax.experimental.pallas import tpu as pltpu
from jax.sharding import PartitionSpec as P

ROWS = 576
COLS = 2048
MATS = 8
ITERS = 3
N_FSDP = 16
OWN = ROWS // N_FSDP
PAD = 40
SIDE = 256
STEM = 32
TAIL = OWN - STEM
NX, NY = 4, 8
N_REP = NX * NY
CHUNK = 512
SHARE = 8
WIDE = COLS // SHARE
SIDES = WIDE // 128
TALL_PIECE = OWN * SIDES

EPSILON = 1e-07
MOMENTUM_BETA = 0.95
QUINTIC_A = 3.4445
QUINTIC_B = -4.775
QUINTIC_C = 2.0315

f32, bf16 = jnp.float32, jnp.bfloat16


def member(group):
    return group // NY * 2 + group % 2


def teams():
    return [[x * NY + y + b for x in range(NX) for b in range(2)] for y in range(0, NY, 2)]


def split(value):
    high = value.astype(bf16)
    low = (value - high.astype(f32)).astype(bf16)
    return high, low


def dot(left, right):
    return jnp.dot(left, right, preferred_element_type=f32)


def dot_nt(left, right):
    return lax.dot_general(left, right, (((1,), (1,)), ((), ())), preferred_element_type=f32)


def product(left, right):
    (lh, ll), (rh, rl) = left, right
    deep = 2 * SIDE
    ends = jnp.concatenate([lh[:, deep:], ll[:, deep:], lh[:, deep:]], axis=1)
    tops = jnp.concatenate([rl[deep:], rh[deep:], rh[deep:]], axis=0)
    lh, ll, rh, rl = lh[:, :deep], ll[:, :deep], rh[:deep], rl[:deep]
    return ((dot(lh, rl) + dot(ll, rh)) + dot(ends, tops)) + dot(lh, rh)


def mirror(top, middle, bottom):
    first = jnp.concatenate([top, bottom[:, :SIDE].T], axis=1)
    second = jnp.concatenate([top[:, SIDE:].T, middle, bottom[:, SIDE : 2 * SIDE].T], axis=1)
    return jnp.concatenate([first, second, bottom], axis=0)


BLOCKS = ((0, SIDE, 0, 2 * SIDE), (SIDE, 2 * SIDE, SIDE, 2 * SIDE), (2 * SIDE, ROWS, 0, ROWS))


def symmetric_product(left, right):
    (lh, ll), (rh, rl) = left, right
    return mirror(
        *[product((lh[a:b], ll[a:b]), (rh[:, c:d], rl[:, c:d])) for a, b, c, d in BLOCKS]
    )


def square(halves):
    high, low = halves
    cross = dot(high, low)
    return (cross + cross.T) + mirror(*[dot(high[a:b], high[:, c:d]) for a, b, c, d in BLOCKS])


def thin_product(rows, halves):
    high, low = halves
    kept = rows.astype(bf16).astype(f32)
    stacked = jnp.concatenate([kept, rows - kept], axis=0).astype(bf16)
    first = dot(stacked, high)
    second = dot(stacked[:PAD], low)
    return first[:PAD] + (first[PAD:] + second)


def orthogonal_kernel(me_ref, s_hbm, u_ref, stem_ref, tail_ref, high_ref, low_ref, sems):
    chunks = COLS // CHUNK
    blocks = CHUNK // 128

    def fetch(part):
        rows = pl.ds(part * blocks * STEM, blocks * STEM)
        return pltpu.make_async_copy(s_hbm.at[:, rows, :], stem_ref.at[part], sems.at[part])

    tails = pl.ds(COLS // 128 * STEM, COLS // 128 * TAIL)
    fetch_tails = pltpu.make_async_copy(s_hbm.at[:, tails, :], tail_ref, sems.at[chunks])
    fetch_tails.start()
    for part in range(chunks):
        fetch(part).start()
    fetch_tails.wait()
    gram = None
    cross = None
    for part in range(chunks):
        fetch(part).wait()
        columns = []
        for inner in range(blocks):
            stem = stem_ref[part, :, inner * STEM : (inner + 1) * STEM, :].reshape(N_FSDP * STEM, 128)
            first = (part * blocks + inner) * TAIL
            tail = [tail_ref[device, first : first + TAIL, :] for device in range(N_FSDP)]
            columns.append(jnp.concatenate([stem] + tail, axis=0))
        high, low = split(jnp.concatenate(columns, axis=1))
        high_ref[part] = high
        low_ref[part] = low
        more_cross, more = dot_nt(high, low), dot_nt(high, high)
        cross = more_cross if part == 0 else cross + more_cross
        gram = more if part == 0 else gram + more
    gram = gram + (cross + cross.T)

    row = lax.broadcasted_iota(jnp.int32, (ROWS, ROWS), 0)
    col = lax.broadcasted_iota(jnp.int32, (ROWS, ROWS), 1)
    diagonal = row == col
    total = jnp.sum(jnp.where(diagonal, gram, 0.0), axis=(0, 1), keepdims=True)
    inverse = 1.0 / (jnp.sqrt(total) + EPSILON)
    finite = inverse > 0.0
    g0 = jnp.where(finite, gram * inverse * inverse, 0.0)
    g0s = split(g0)
    q1s = split(jnp.where(diagonal, QUINTIC_A, 0.0) + QUINTIC_B * g0 + QUINTIC_C * square(g0s))
    g1s = split(symmetric_product(g0s, split(square(q1s))))

    def by_g1(rows):
        return thin_product(rows, g1s)

    def quintic(rows, once, twice):
        return QUINTIC_A * rows + QUINTIC_B * once + QUINTIC_C * twice

    def by_q2(rows):
        once = by_g1(rows)
        return quintic(rows, once, by_g1(once))

    def by_g2(rows):
        return by_q2(by_q2(by_g1(rows)))

    local = lax.broadcasted_iota(jnp.int32, (PAD, ROWS), 0)
    here = lax.broadcasted_iota(jnp.int32, (PAD, ROWS), 1)
    in_stem = me_ref[0] * STEM + local
    in_tail = N_FSDP * STEM + me_ref[0] * TAIL + local - STEM
    own = jnp.where(local < STEM, in_stem, jnp.where(local < OWN, in_tail, -1))
    unit = jnp.where(own == here, 1.0, 0.0)
    mixed = thin_product(by_q2(unit), q1s)
    once = by_g2(mixed)
    mixed = quintic(mixed, once, by_g2(once))
    factor = 0.2 * math.sqrt(max(ROWS, COLS))
    for part in range(chunks):
        update = thin_product(mixed, (high_ref[part], low_ref[part])) * inverse * factor
        update = jnp.where(finite, update, 0.0)
        for inner in range(CHUNK // WIDE):
            lane = inner * WIDE
            sides = [update[:OWN, lane + side * 128 : lane + (side + 1) * 128] for side in range(SIDES)]
            piece = jnp.concatenate(sides, axis=0).astype(bf16)
            for group in range(N_REP):
                if member(group) == part * (CHUNK // WIDE) + inner:
                    u_ref[group] = piece


def orthogonal_rows(position, whole):
    chunks = COLS // CHUNK
    return pl.pallas_call(
        orthogonal_kernel,
        out_shape=jax.ShapeDtypeStruct((N_REP, TALL_PIECE, 128), bf16),
        in_specs=[
            pl.BlockSpec(memory_space=pltpu.SMEM),
            pl.BlockSpec(memory_space=pltpu.HBM),
        ],
        out_specs=pl.BlockSpec(memory_space=pltpu.VMEM),
        scratch_shapes=[
            pltpu.VMEM((chunks, N_FSDP, CHUNK // 128 * STEM, 128), f32),
            pltpu.VMEM((N_FSDP, COLS // 128 * TAIL, 128), f32),
            pltpu.VMEM((chunks, ROWS, CHUNK), bf16),
            pltpu.VMEM((chunks, ROWS, CHUNK), bf16),
            pltpu.SemaphoreType.DMA((chunks + 1,)),
        ],
        compiler_params=pltpu.CompilerParams(vmem_limit_bytes=48 * 1024 * 1024),
    )(position, whole)


def choose_kernel(owners_ref, arrived_ref, out_ref, rows_ref):
    for mat in range(MATS):
        rows_ref[pl.ds(mat, TALL_PIECE, stride=MATS), :] = arrived_ref[owners_ref[mat]].astype(f32)
    rows = rows_ref[...].astype(bf16)
    for copy in range(SHARE):
        out_ref[copy] = rows


def choose(owners, arrived):
    return pl.pallas_call(
        choose_kernel,
        out_shape=jax.ShapeDtypeStruct((SHARE, TALL_PIECE * MATS, 128), bf16),
        in_specs=[pl.BlockSpec(memory_space=pltpu.SMEM), pl.BlockSpec(memory_space=pltpu.VMEM)],
        out_specs=pl.BlockSpec(memory_space=pltpu.VMEM),
        scratch_shapes=[pltpu.VMEM((TALL_PIECE * MATS, 128), f32)],
        compiler_params=pltpu.CompilerParams(vmem_limit_bytes=16 * 1024 * 1024),
    )(owners, arrived)


def assemble_kernel(parts_ref, out_hbm, rows_ref, sems):
    half = OWN // 2

    def store(step):
        rows = pl.ds(step * half, half)
        return pltpu.make_async_copy(rows_ref.at[rows], out_hbm.at[rows], sems.at[step])

    for step in range(2):
        for part in range(SHARE):
            for side in range(SIDES):
                lane = part * WIDE + side * 128
                first = side * OWN + step * half
                rows_ref[step * half : (step + 1) * half, :, lane : lane + 128] = parts_ref[part, first : first + half]
        store(step).start()
    for step in range(2):
        store(step).wait()


def assemble(parts):
    return pl.pallas_call(
        assemble_kernel,
        out_shape=pltpu.HBM((OWN, MATS, COLS), bf16),
        in_specs=[pl.BlockSpec(memory_space=pltpu.VMEM)],
        out_specs=pl.BlockSpec(memory_space=pltpu.HBM),
        scratch_shapes=[pltpu.VMEM((OWN, MATS, COLS), bf16), pltpu.SemaphoreType.DMA((2,))],
        compiler_params=pltpu.CompilerParams(vmem_limit_bytes=32 * 1024 * 1024),
    )(parts)


def steer_kernel(
    group_ref, owners_hbm, grads_hbm, momentum_hbm, renewed_ref, steered_ref,
    owners_ref, grads_ref, momentum_ref, wide_ref, fresh_ref, sems,
):
    blocks = COLS // 128
    chunks = COLS // CHUNK

    def fetch(part):
        lanes = pl.ds(part * CHUNK, CHUNK)
        return pltpu.make_async_copy(grads_hbm.at[:, :, lanes], grads_ref.at[part], sems.at[part])

    fetch_owners = pltpu.make_async_copy(owners_hbm, owners_ref, sems.at[chunks])
    held_rows = pl.ds(0, OWN * blocks)
    fetch_momentum = pltpu.make_async_copy(momentum_hbm, momentum_ref.at[held_rows], sems.at[chunks + 1])
    fetch_owners.start()
    fetch_momentum.start()
    for part in range(chunks):
        fetch(part).start()
    fetch_owners.wait()
    owns_one = owners_ref[0] == group_ref[0]
    chosen = 0
    for index in range(1, MATS):
        here = owners_ref[index] == group_ref[0]
        owns_one = jnp.logical_or(owns_one, here)
        chosen = chosen + jnp.where(here, index, 0)
    fetch_momentum.wait()
    for block in range(blocks):
        part, inner = block // (CHUNK // 128), block % (CHUNK // 128)
        if inner == 0:
            fetch(part).wait()
        wide = grads_ref[part, :, :, inner * 128 : (inner + 1) * 128].astype(f32)
        wide_ref[block, : OWN * MATS, :] = wide.reshape(OWN * MATS, 128)
        gradient = wide_ref[block, pl.ds(chosen, PAD, stride=MATS), :]
        held_state = momentum_ref[pl.ds(block, PAD, stride=blocks), :]
        renewed = jnp.where(owns_one, MOMENTUM_BETA * held_state + gradient, held_state)
        fresh_ref[pl.ds(block, PAD, stride=blocks), :] = renewed
        steered = gradient + MOMENTUM_BETA * renewed
        steered_ref[block * STEM : (block + 1) * STEM, :] = steered[:STEM]
        first = blocks * STEM + block * TAIL
        steered_ref[first : first + TAIL, :] = steered[STEM:OWN]
    renewed_ref[...] = fresh_ref[: OWN * blocks, :]


def in_hbm(value):
    return pltpu.with_memory_space_constraint(value, pltpu.HBM)


def steer(owners, group, grads, momentum):
    chunks = COLS // CHUNK
    return pl.pallas_call(
        steer_kernel,
        in_specs=[pl.BlockSpec(memory_space=pltpu.SMEM)] + [pl.BlockSpec(memory_space=pltpu.HBM)] * 3,
        out_specs=[pl.BlockSpec(memory_space=pltpu.VMEM)] * 2,
        out_shape=[
            jax.ShapeDtypeStruct((OWN * COLS // 128, 128), f32),
            jax.ShapeDtypeStruct((OWN * COLS // 128, 128), f32),
        ],
        scratch_shapes=[
            pltpu.SMEM((MATS,), jnp.int32),
            pltpu.VMEM((chunks, OWN, MATS, CHUNK), bf16),
            pltpu.VMEM((PAD * COLS // 128, 128), f32),
            pltpu.VMEM((COLS // 128, PAD * MATS, 128), f32),
            pltpu.VMEM((PAD * COLS // 128, 128), f32),
            pltpu.SemaphoreType.DMA((chunks + 2,)),
        ],
        compiler_params=pltpu.CompilerParams(vmem_limit_bytes=32 * 1024 * 1024),
    )(group, in_hbm(owners), in_hbm(grads), in_hbm(momentum))


def deliver(pieces, owners):
    arrived = lax.all_to_all(pieces, "rep", split_axis=0, concat_axis=0, tiled=True)
    copies = choose(owners, arrived)
    parts = lax.all_to_all(copies, "rep", split_axis=0, concat_axis=0, tiled=True, axis_index_groups=teams())
    rows = assemble(parts.reshape(SHARE, TALL_PIECE, MATS, 128))
    return rows.transpose(1, 0, 2)


def shards(grads, momentum, owners):
    group = lax.axis_index("rep").astype(jnp.int32)[None]
    position = lax.axis_index("fsdp").astype(jnp.int32)[None]
    flat = momentum.reshape(OWN * COLS // 128, 128)
    renewed, steered = steer(owners, group, grads.transpose(1, 0, 2), flat)
    whole = lax.all_gather(steered, "fsdp")
    pieces = orthogonal_rows(position, in_hbm(whole))
    update = deliver(pieces, owners)
    return (update, renewed.reshape(1, OWN, COLS))


def solution(mesh):
    in_specs = (P(None, "fsdp", None), P("rep", "fsdp", None), P())
    out_specs = (P(None, "fsdp", None), P("rep", "fsdp", None))
    return jax.shard_map(shards, mesh=mesh, in_specs=in_specs, out_specs=out_specs, check_vma=False)
```

```python
import math

import jax
import jax.numpy as jnp
from jax import lax
from jax.experimental import pallas as pl
from jax.experimental.pallas import tpu as pltpu
from jax.sharding import PartitionSpec as P

ROWS = 576
COLS = 2048
MATS = 8
ITERS = 3
N_FSDP = 16
OWN = ROWS // N_FSDP
PAD = 40
SIDE = 256
STEM = 32
TAIL = OWN - STEM
NX, NY = 4, 8
N_REP = NX * NY
CHUNK = 512
SHARE = 8
WIDE = COLS // SHARE
SIDES = WIDE // 128
TALL_PIECE = OWN * SIDES

EPSILON = 1e-07
MOMENTUM_BETA = 0.95
QUINTIC_A = 3.4445
QUINTIC_B = -4.775
QUINTIC_C = 2.0315

f32, bf16 = jnp.float32, jnp.bfloat16


def member(group):
    return group // NY * 2 + group % 2


def teams():
    return [[x * NY + y + b for x in range(NX) for b in range(2)] for y in range(0, NY, 2)]


def split(value):
    high = value.astype(bf16)
    low = (value - high.astype(f32)).astype(bf16)
    return high, low


def dot(left, right):
    return jnp.dot(left, right, preferred_element_type=f32)


def dot_nt(left, right):
    return lax.dot_general(left, right, (((1,), (1,)), ((), ())), preferred_element_type=f32)


def product(left, right):
    (lh, ll), (rh, rl) = left, right
    deep = 2 * SIDE
    ends = jnp.concatenate([lh[:, deep:], ll[:, deep:], lh[:, deep:]], axis=1)
    tops = jnp.concatenate([rl[deep:], rh[deep:], rh[deep:]], axis=0)
    lh, ll, rh, rl = lh[:, :deep], ll[:, :deep], rh[:deep], rl[:deep]
    return ((dot(lh, rl) + dot(ll, rh)) + dot(ends, tops)) + dot(lh, rh)


def mirror(top, middle, bottom):
    first = jnp.concatenate([top, bottom[:, :SIDE].T], axis=1)
    second = jnp.concatenate([top[:, SIDE:].T, middle, bottom[:, SIDE : 2 * SIDE].T], axis=1)
    return jnp.concatenate([first, second, bottom], axis=0)


BLOCKS = ((0, SIDE, 0, 2 * SIDE), (SIDE, 2 * SIDE, SIDE, 2 * SIDE), (2 * SIDE, ROWS, 0, ROWS))


def symmetric_product(left, right):
    (lh, ll), (rh, rl) = left, right
    return mirror(
        *[product((lh[a:b], ll[a:b]), (rh[:, c:d], rl[:, c:d])) for a, b, c, d in BLOCKS]
    )


def square(halves):
    high, low = halves
    cross = dot(high, low)
    return (cross + cross.T) + mirror(*[dot(high[a:b], high[:, c:d]) for a, b, c, d in BLOCKS])


def thin_product(rows, halves):
    high, low = halves
    kept = rows.astype(bf16).astype(f32)
    stacked = jnp.concatenate([kept, rows - kept], axis=0).astype(bf16)
    first = dot(stacked, high)
    second = dot(stacked[:PAD], low)
    return first[:PAD] + (first[PAD:] + second)


def orthogonal_kernel(me_ref, s_hbm, u_ref, stem_ref, tail_ref, high_ref, low_ref, sems):
    chunks = COLS // CHUNK
    blocks = CHUNK // 128

    def fetch(part):
        rows = pl.ds(part * blocks * STEM, blocks * STEM)
        return pltpu.make_async_copy(s_hbm.at[:, rows, :], stem_ref.at[part], sems.at[part])

    tails = pl.ds(COLS // 128 * STEM, COLS // 128 * TAIL)
    fetch_tails = pltpu.make_async_copy(s_hbm.at[:, tails, :], tail_ref, sems.at[chunks])
    fetch_tails.start()
    for part in range(chunks):
        fetch(part).start()
    fetch_tails.wait()
    gram = None
    cross = None
    for part in range(chunks):
        fetch(part).wait()
        columns = []
        for inner in range(blocks):
            stem = stem_ref[part, :, inner * STEM : (inner + 1) * STEM, :].reshape(N_FSDP * STEM, 128)
            first = (part * blocks + inner) * TAIL
            tail = [tail_ref[device, first : first + TAIL, :] for device in range(N_FSDP)]
            columns.append(jnp.concatenate([stem] + tail, axis=0))
        high, low = split(jnp.concatenate(columns, axis=1))
        high_ref[part] = high
        low_ref[part] = low
        more_cross, more = dot_nt(high, low), dot_nt(high, high)
        cross = more_cross if part == 0 else cross + more_cross
        gram = more if part == 0 else gram + more
    gram = gram + (cross + cross.T)

    row = lax.broadcasted_iota(jnp.int32, (ROWS, ROWS), 0)
    col = lax.broadcasted_iota(jnp.int32, (ROWS, ROWS), 1)
    diagonal = row == col
    total = jnp.sum(jnp.where(diagonal, gram, 0.0), axis=(0, 1), keepdims=True)
    inverse = 1.0 / (jnp.sqrt(total) + EPSILON)
    finite = inverse > 0.0
    g0 = jnp.where(finite, gram * inverse * inverse, 0.0)
    g0s = split(g0)
    q1s = split(jnp.where(diagonal, QUINTIC_A, 0.0) + QUINTIC_B * g0 + QUINTIC_C * square(g0s))
    g1s = split(symmetric_product(g0s, split(square(q1s))))

    def by_g1(rows):
        return thin_product(rows, g1s)

    def quintic(rows, once, twice):
        return QUINTIC_A * rows + QUINTIC_B * once + QUINTIC_C * twice

    def by_q2(rows):
        once = by_g1(rows)
        return quintic(rows, once, by_g1(once))

    def by_g2(rows):
        return by_q2(by_q2(by_g1(rows)))

    local = lax.broadcasted_iota(jnp.int32, (PAD, ROWS), 0)
    here = lax.broadcasted_iota(jnp.int32, (PAD, ROWS), 1)
    in_stem = me_ref[0] * STEM + local
    in_tail = N_FSDP * STEM + me_ref[0] * TAIL + local - STEM
    own = jnp.where(local < STEM, in_stem, jnp.where(local < OWN, in_tail, -1))
    unit = jnp.where(own == here, 1.0, 0.0)
    mixed = thin_product(by_q2(unit), q1s)
    once = by_g2(mixed)
    mixed = quintic(mixed, once, by_g2(once))
    factor = 0.2 * math.sqrt(max(ROWS, COLS))
    for part in range(chunks):
        update = thin_product(mixed, (high_ref[part], low_ref[part])) * inverse * factor
        update = jnp.where(finite, update, 0.0)
        for inner in range(CHUNK // WIDE):
            lane = inner * WIDE
            sides = [update[:OWN, lane + side * 128 : lane + (side + 1) * 128] for side in range(SIDES)]
            piece = jnp.concatenate(sides, axis=0).astype(bf16)
            for group in range(N_REP):
                if member(group) == part * (CHUNK // WIDE) + inner:
                    u_ref[group] = piece


def orthogonal_rows(position, whole):
    chunks = COLS // CHUNK
    return pl.pallas_call(
        orthogonal_kernel,
        out_shape=jax.ShapeDtypeStruct((N_REP, TALL_PIECE, 128), bf16),
        in_specs=[
            pl.BlockSpec(memory_space=pltpu.SMEM),
            pl.BlockSpec(memory_space=pltpu.HBM),
        ],
        out_specs=pl.BlockSpec(memory_space=pltpu.VMEM),
        scratch_shapes=[
            pltpu.VMEM((chunks, N_FSDP, CHUNK // 128 * STEM, 128), f32),
            pltpu.VMEM((N_FSDP, COLS // 128 * TAIL, 128), f32),
            pltpu.VMEM((chunks, ROWS, CHUNK), bf16),
            pltpu.VMEM((chunks, ROWS, CHUNK), bf16),
            pltpu.SemaphoreType.DMA((chunks + 1,)),
        ],
        compiler_params=pltpu.CompilerParams(vmem_limit_bytes=48 * 1024 * 1024),
    )(position, whole)


def choose_kernel(owners_ref, arrived_ref, out_ref, rows_ref):
    for mat in range(MATS):
        rows_ref[pl.ds(mat, TALL_PIECE, stride=MATS), :] = arrived_ref[owners_ref[mat]].astype(f32)
    rows = rows_ref[...].astype(bf16)
    for copy in range(SHARE):
        out_ref[copy] = rows


def choose(owners, arrived):
    return pl.pallas_call(
        choose_kernel,
        out_shape=jax.ShapeDtypeStruct((SHARE, TALL_PIECE * MATS, 128), bf16),
        in_specs=[pl.BlockSpec(memory_space=pltpu.SMEM), pl.BlockSpec(memory_space=pltpu.VMEM)],
        out_specs=pl.BlockSpec(memory_space=pltpu.VMEM),
        scratch_shapes=[pltpu.VMEM((TALL_PIECE * MATS, 128), f32)],
        compiler_params=pltpu.CompilerParams(vmem_limit_bytes=16 * 1024 * 1024),
    )(owners, arrived)


def assemble_kernel(parts_ref, out_hbm, rows_ref, sems):
    half = OWN // 2

    def store(step):
        rows = pl.ds(step * half, half)
        return pltpu.make_async_copy(rows_ref.at[rows], out_hbm.at[rows], sems.at[step])

    for step in range(2):
        for part in range(SHARE):
            for side in range(SIDES):
                lane = part * WIDE + side * 128
                first = side * OWN + step * half
                rows_ref[step * half : (step + 1) * half, :, lane : lane + 128] = parts_ref[part, first : first + half]
        store(step).start()
    for step in range(2):
        store(step).wait()


def assemble(parts):
    return pl.pallas_call(
        assemble_kernel,
        out_shape=pltpu.HBM((OWN, MATS, COLS), bf16),
        in_specs=[pl.BlockSpec(memory_space=pltpu.VMEM)],
        out_specs=pl.BlockSpec(memory_space=pltpu.HBM),
        scratch_shapes=[pltpu.VMEM((OWN, MATS, COLS), bf16), pltpu.SemaphoreType.DMA((2,))],
        compiler_params=pltpu.CompilerParams(vmem_limit_bytes=32 * 1024 * 1024),
    )(parts)


def steer_kernel(
    group_ref, owners_hbm, grads_hbm, momentum_hbm, steered_ref,
    owners_ref, grads_ref, momentum_ref, wide_ref, sems,
):
    blocks = COLS // 128
    chunks = COLS // CHUNK

    def fetch(part):
        lanes = pl.ds(part * CHUNK, CHUNK)
        return pltpu.make_async_copy(grads_hbm.at[:, :, lanes], grads_ref.at[part], sems.at[part])

    fetch_owners = pltpu.make_async_copy(owners_hbm, owners_ref, sems.at[chunks])
    held_rows = pl.ds(0, OWN * blocks)
    fetch_momentum = pltpu.make_async_copy(momentum_hbm, momentum_ref.at[held_rows], sems.at[chunks + 1])
    fetch_owners.start()
    fetch_momentum.start()
    for part in range(chunks):
        fetch(part).start()
    fetch_owners.wait()
    owns_one = owners_ref[0] == group_ref[0]
    chosen = 0
    for index in range(1, MATS):
        here = owners_ref[index] == group_ref[0]
        owns_one = jnp.logical_or(owns_one, here)
        chosen = chosen + jnp.where(here, index, 0)
    fetch_momentum.wait()
    for block in range(blocks):
        part, inner = block // (CHUNK // 128), block % (CHUNK // 128)
        if inner == 0:
            fetch(part).wait()
        wide = grads_ref[part, :, :, inner * 128 : (inner + 1) * 128].astype(f32)
        wide_ref[block, : OWN * MATS, :] = wide.reshape(OWN * MATS, 128)
        gradient = wide_ref[block, pl.ds(chosen, PAD, stride=MATS), :]
        held_state = momentum_ref[pl.ds(block, PAD, stride=blocks), :]
        renewed = jnp.where(owns_one, MOMENTUM_BETA * held_state + gradient, held_state)
        steered = gradient + MOMENTUM_BETA * renewed
        steered_ref[block * STEM : (block + 1) * STEM, :] = steered[:STEM]
        first = blocks * STEM + block * TAIL
        steered_ref[first : first + TAIL, :] = steered[STEM:OWN]


def renew_kernel(
    group_ref, owners_hbm, grads_hbm, momentum_hbm, steered_hbm, renewed_ref,
    owners_ref, grads_ref, momentum_ref, wide_ref, fresh_ref, sems,
):
    blocks = COLS // 128
    chunks = COLS // CHUNK

    def fetch(part):
        lanes = pl.ds(part * CHUNK, CHUNK)
        return pltpu.make_async_copy(grads_hbm.at[:, :, lanes], grads_ref.at[part], sems.at[part])

    fetch_owners = pltpu.make_async_copy(owners_hbm, owners_ref, sems.at[chunks])
    held_rows = pl.ds(0, OWN * blocks)
    fetch_momentum = pltpu.make_async_copy(momentum_hbm, momentum_ref.at[held_rows], sems.at[chunks + 1])
    fetch_owners.start()
    fetch_momentum.start()
    for part in range(chunks):
        fetch(part).start()
    fetch_owners.wait()
    owns_one = owners_ref[0] == group_ref[0]
    chosen = 0
    for index in range(1, MATS):
        here = owners_ref[index] == group_ref[0]
        owns_one = jnp.logical_or(owns_one, here)
        chosen = chosen + jnp.where(here, index, 0)
    fetch_momentum.wait()
    for block in range(blocks):
        part, inner = block // (CHUNK // 128), block % (CHUNK // 128)
        if inner == 0:
            fetch(part).wait()
        wide = grads_ref[part, :, :, inner * 128 : (inner + 1) * 128].astype(f32)
        wide_ref[block, : OWN * MATS, :] = wide.reshape(OWN * MATS, 128)
        gradient = wide_ref[block, pl.ds(chosen, PAD, stride=MATS), :]
        held_state = momentum_ref[pl.ds(block, PAD, stride=blocks), :]
        renewed = jnp.where(owns_one, MOMENTUM_BETA * held_state + gradient, held_state)
        fresh_ref[pl.ds(block, PAD, stride=blocks), :] = renewed
    renewed_ref[...] = fresh_ref[: OWN * blocks, :]


def in_hbm(value):
    return pltpu.with_memory_space_constraint(value, pltpu.HBM)


def read_scratch(*more):
    chunks = COLS // CHUNK
    return [
        pltpu.SMEM((MATS,), jnp.int32),
        pltpu.VMEM((chunks, OWN, MATS, CHUNK), bf16),
        pltpu.VMEM((PAD * COLS // 128, 128), f32),
        pltpu.VMEM((COLS // 128, PAD * MATS, 128), f32),
        *more,
        pltpu.SemaphoreType.DMA((chunks + 2,)),
    ]


def steer(owners, group, grads, momentum):
    return pl.pallas_call(
        steer_kernel,
        in_specs=[pl.BlockSpec(memory_space=pltpu.SMEM)] + [pl.BlockSpec(memory_space=pltpu.HBM)] * 3,
        out_specs=pl.BlockSpec(memory_space=pltpu.VMEM),
        out_shape=jax.ShapeDtypeStruct((OWN * COLS // 128, 128), f32),
        scratch_shapes=read_scratch(),
        compiler_params=pltpu.CompilerParams(vmem_limit_bytes=32 * 1024 * 1024),
    )(group, in_hbm(owners), in_hbm(grads), in_hbm(momentum))


def renew(owners, group, grads, momentum, steered):
    return pl.pallas_call(
        renew_kernel,
        in_specs=[pl.BlockSpec(memory_space=pltpu.SMEM)]
        + [pl.BlockSpec(memory_space=pltpu.HBM)] * 3
        + [pl.BlockSpec(memory_space=pl.ANY)],
        out_specs=pl.BlockSpec(memory_space=pltpu.VMEM),
        out_shape=jax.ShapeDtypeStruct((OWN * COLS // 128, 128), f32),
        scratch_shapes=read_scratch(pltpu.VMEM((PAD * COLS // 128, 128), f32)),
        compiler_params=pltpu.CompilerParams(vmem_limit_bytes=32 * 1024 * 1024),
    )(group, in_hbm(owners), in_hbm(grads), in_hbm(momentum), steered)


def deliver(pieces, owners):
    arrived = lax.all_to_all(pieces, "rep", split_axis=0, concat_axis=0, tiled=True)
    copies = choose(owners, arrived)
    parts = lax.all_to_all(copies, "rep", split_axis=0, concat_axis=0, tiled=True, axis_index_groups=teams())
    rows = assemble(parts.reshape(SHARE, TALL_PIECE, MATS, 128))
    return rows.transpose(1, 0, 2)


def shards(grads, momentum, owners):
    group = lax.axis_index("rep").astype(jnp.int32)[None]
    position = lax.axis_index("fsdp").astype(jnp.int32)[None]
    flat = momentum.reshape(OWN * COLS // 128, 128)
    by_row = grads.transpose(1, 0, 2)
    steered = steer(owners, group, by_row, flat)
    renewed = renew(owners, group, by_row, flat, steered)
    whole = lax.all_gather(steered, "fsdp")
    pieces = orthogonal_rows(position, in_hbm(whole))
    update = deliver(pieces, owners)
    return (update, renewed.reshape(1, OWN, COLS))


def solution(mesh):
    in_specs = (P(None, "fsdp", None), P("rep", "fsdp", None), P())
    out_specs = (P(None, "fsdp", None), P("rep", "fsdp", None))
    return jax.shard_map(shards, mesh=mesh, in_specs=in_specs, out_specs=out_specs, check_vma=False)
```

```python
import math

import jax
import jax.numpy as jnp
from jax import lax
from jax.experimental import pallas as pl
from jax.experimental.pallas import tpu as pltpu
from jax.sharding import PartitionSpec as P

ROWS = 576
COLS = 2048
MATS = 8
ITERS = 3
N_FSDP = 16
OWN = ROWS // N_FSDP
PAD = 40
SIDE = 256
STEM = 32
TAIL = OWN - STEM
NX, NY = 4, 8
N_REP = NX * NY
CHUNK = 512
SHARE = 8
WIDE = COLS // SHARE
SIDES = WIDE // 128
TALL_PIECE = OWN * SIDES

EPSILON = 1e-07
MOMENTUM_BETA = 0.95
QUINTIC_A = 3.4445
QUINTIC_B = -4.775
QUINTIC_C = 2.0315

f32, bf16 = jnp.float32, jnp.bfloat16


def member(group):
    return group // NY * 2 + group % 2


def teams():
    return [[x * NY + y + b for x in range(NX) for b in range(2)] for y in range(0, NY, 2)]


def split(value):
    high = value.astype(bf16)
    low = (value - high.astype(f32)).astype(bf16)
    return high, low


def dot(left, right):
    return jnp.dot(left, right, preferred_element_type=f32)


def dot_nt(left, right):
    return lax.dot_general(left, right, (((1,), (1,)), ((), ())), preferred_element_type=f32)


def product(left, right):
    (lh, ll), (rh, rl) = left, right
    deep = 2 * SIDE
    ends = jnp.concatenate([lh[:, deep:], ll[:, deep:], lh[:, deep:]], axis=1)
    tops = jnp.concatenate([rl[deep:], rh[deep:], rh[deep:]], axis=0)
    lh, ll, rh, rl = lh[:, :deep], ll[:, :deep], rh[:deep], rl[:deep]
    return ((dot(lh, rl) + dot(ll, rh)) + dot(ends, tops)) + dot(lh, rh)


def mirror(top, middle, bottom):
    first = jnp.concatenate([top, bottom[:, :SIDE].T], axis=1)
    second = jnp.concatenate([top[:, SIDE:].T, middle, bottom[:, SIDE : 2 * SIDE].T], axis=1)
    return jnp.concatenate([first, second, bottom], axis=0)


BLOCKS = ((0, SIDE, 0, 2 * SIDE), (SIDE, 2 * SIDE, SIDE, 2 * SIDE), (2 * SIDE, ROWS, 0, ROWS))


def symmetric_product(left, right):
    (lh, ll), (rh, rl) = left, right
    return mirror(
        *[product((lh[a:b], ll[a:b]), (rh[:, c:d], rl[:, c:d])) for a, b, c, d in BLOCKS]
    )


def square(halves):
    high, low = halves
    cross = dot(high, low)
    return (cross + cross.T) + mirror(*[dot(high[a:b], high[:, c:d]) for a, b, c, d in BLOCKS])


def thin_product(rows, halves):
    high, low = halves
    kept = rows.astype(bf16).astype(f32)
    stacked = jnp.concatenate([kept, rows - kept], axis=0).astype(bf16)
    first = dot(stacked, high)
    second = dot(stacked[:PAD], low)
    return first[:PAD] + (first[PAD:] + second)


def orthogonal_kernel(me_ref, s_hbm, renewed_hbm, u_ref, stem_ref, tail_ref, high_ref, low_ref, sems):
    chunks = COLS // CHUNK
    blocks = CHUNK // 128

    def fetch(part):
        rows = pl.ds(part * blocks * STEM, blocks * STEM)
        return pltpu.make_async_copy(s_hbm.at[:, rows, :], stem_ref.at[part], sems.at[part])

    tails = pl.ds(COLS // 128 * STEM, COLS // 128 * TAIL)
    fetch_tails = pltpu.make_async_copy(s_hbm.at[:, tails, :], tail_ref, sems.at[chunks])
    fetch_tails.start()
    for part in range(chunks):
        fetch(part).start()
    fetch_tails.wait()
    gram = None
    cross = None
    for part in range(chunks):
        fetch(part).wait()
        columns = []
        for inner in range(blocks):
            stem = stem_ref[part, :, inner * STEM : (inner + 1) * STEM, :].reshape(N_FSDP * STEM, 128)
            first = (part * blocks + inner) * TAIL
            tail = [tail_ref[device, first : first + TAIL, :] for device in range(N_FSDP)]
            columns.append(jnp.concatenate([stem] + tail, axis=0))
        high, low = split(jnp.concatenate(columns, axis=1))
        high_ref[part] = high
        low_ref[part] = low
        more_cross, more = dot_nt(high, low), dot_nt(high, high)
        cross = more_cross if part == 0 else cross + more_cross
        gram = more if part == 0 else gram + more
    gram = gram + (cross + cross.T)

    row = lax.broadcasted_iota(jnp.int32, (ROWS, ROWS), 0)
    col = lax.broadcasted_iota(jnp.int32, (ROWS, ROWS), 1)
    diagonal = row == col
    total = jnp.sum(jnp.where(diagonal, gram, 0.0), axis=(0, 1), keepdims=True)
    inverse = 1.0 / (jnp.sqrt(total) + EPSILON)
    finite = inverse > 0.0
    g0 = jnp.where(finite, gram * inverse * inverse, 0.0)
    g0s = split(g0)
    q1s = split(jnp.where(diagonal, QUINTIC_A, 0.0) + QUINTIC_B * g0 + QUINTIC_C * square(g0s))
    g1s = split(symmetric_product(g0s, split(square(q1s))))

    def by_g1(rows):
        return thin_product(rows, g1s)

    def quintic(rows, once, twice):
        return QUINTIC_A * rows + QUINTIC_B * once + QUINTIC_C * twice

    def by_q2(rows):
        once = by_g1(rows)
        return quintic(rows, once, by_g1(once))

    def by_g2(rows):
        return by_q2(by_q2(by_g1(rows)))

    local = lax.broadcasted_iota(jnp.int32, (PAD, ROWS), 0)
    here = lax.broadcasted_iota(jnp.int32, (PAD, ROWS), 1)
    in_stem = me_ref[0] * STEM + local
    in_tail = N_FSDP * STEM + me_ref[0] * TAIL + local - STEM
    own = jnp.where(local < STEM, in_stem, jnp.where(local < OWN, in_tail, -1))
    unit = jnp.where(own == here, 1.0, 0.0)
    mixed = thin_product(by_q2(unit), q1s)
    once = by_g2(mixed)
    mixed = quintic(mixed, once, by_g2(once))
    factor = 0.2 * math.sqrt(max(ROWS, COLS))
    for part in range(chunks):
        update = thin_product(mixed, (high_ref[part], low_ref[part])) * inverse * factor
        update = jnp.where(finite, update, 0.0)
        for inner in range(CHUNK // WIDE):
            lane = inner * WIDE
            sides = [update[:OWN, lane + side * 128 : lane + (side + 1) * 128] for side in range(SIDES)]
            piece = jnp.concatenate(sides, axis=0).astype(bf16)
            for group in range(N_REP):
                if member(group) == part * (CHUNK // WIDE) + inner:
                    u_ref[group] = piece


def orthogonal_rows(position, whole, renewed):
    chunks = COLS // CHUNK
    return pl.pallas_call(
        orthogonal_kernel,
        out_shape=jax.ShapeDtypeStruct((N_REP, TALL_PIECE, 128), bf16),
        in_specs=[
            pl.BlockSpec(memory_space=pltpu.SMEM),
            pl.BlockSpec(memory_space=pltpu.HBM),
            pl.BlockSpec(memory_space=pl.ANY),
        ],
        out_specs=pl.BlockSpec(memory_space=pltpu.VMEM),
        scratch_shapes=[
            pltpu.VMEM((chunks, N_FSDP, CHUNK // 128 * STEM, 128), f32),
            pltpu.VMEM((N_FSDP, COLS // 128 * TAIL, 128), f32),
            pltpu.VMEM((chunks, ROWS, CHUNK), bf16),
            pltpu.VMEM((chunks, ROWS, CHUNK), bf16),
            pltpu.SemaphoreType.DMA((chunks + 1,)),
        ],
        compiler_params=pltpu.CompilerParams(vmem_limit_bytes=48 * 1024 * 1024),
    )(position, whole, renewed)


def choose_kernel(owners_ref, arrived_ref, out_ref, rows_ref):
    for mat in range(MATS):
        rows_ref[pl.ds(mat, TALL_PIECE, stride=MATS), :] = arrived_ref[owners_ref[mat]].astype(f32)
    rows = rows_ref[...].astype(bf16)
    for copy in range(SHARE):
        out_ref[copy] = rows


def choose(owners, arrived):
    return pl.pallas_call(
        choose_kernel,
        out_shape=jax.ShapeDtypeStruct((SHARE, TALL_PIECE * MATS, 128), bf16),
        in_specs=[pl.BlockSpec(memory_space=pltpu.SMEM), pl.BlockSpec(memory_space=pltpu.VMEM)],
        out_specs=pl.BlockSpec(memory_space=pltpu.VMEM),
        scratch_shapes=[pltpu.VMEM((TALL_PIECE * MATS, 128), f32)],
        compiler_params=pltpu.CompilerParams(vmem_limit_bytes=16 * 1024 * 1024),
    )(owners, arrived)


def assemble_kernel(parts_ref, out_hbm, rows_ref, sems):
    half = OWN // 2

    def store(step):
        rows = pl.ds(step * half, half)
        return pltpu.make_async_copy(rows_ref.at[rows], out_hbm.at[rows], sems.at[step])

    for step in range(2):
        for part in range(SHARE):
            for side in range(SIDES):
                lane = part * WIDE + side * 128
                first = side * OWN + step * half
                rows_ref[step * half : (step + 1) * half, :, lane : lane + 128] = parts_ref[part, first : first + half]
        store(step).start()
    for step in range(2):
        store(step).wait()


def assemble(parts):
    return pl.pallas_call(
        assemble_kernel,
        out_shape=pltpu.HBM((OWN, MATS, COLS), bf16),
        in_specs=[pl.BlockSpec(memory_space=pltpu.VMEM)],
        out_specs=pl.BlockSpec(memory_space=pltpu.HBM),
        scratch_shapes=[pltpu.VMEM((OWN, MATS, COLS), bf16), pltpu.SemaphoreType.DMA((2,))],
        compiler_params=pltpu.CompilerParams(vmem_limit_bytes=32 * 1024 * 1024),
    )(parts)


def steer_kernel(
    group_ref, owners_hbm, grads_hbm, momentum_hbm, steered_ref,
    owners_ref, grads_ref, momentum_ref, wide_ref, sems,
):
    blocks = COLS // 128
    chunks = COLS // CHUNK

    def fetch(part):
        lanes = pl.ds(part * CHUNK, CHUNK)
        return pltpu.make_async_copy(grads_hbm.at[:, :, lanes], grads_ref.at[part], sems.at[part])

    fetch_owners = pltpu.make_async_copy(owners_hbm, owners_ref, sems.at[chunks])
    held_rows = pl.ds(0, OWN * blocks)
    fetch_momentum = pltpu.make_async_copy(momentum_hbm, momentum_ref.at[held_rows], sems.at[chunks + 1])
    fetch_owners.start()
    fetch_momentum.start()
    for part in range(chunks):
        fetch(part).start()
    fetch_owners.wait()
    owns_one = owners_ref[0] == group_ref[0]
    chosen = 0
    for index in range(1, MATS):
        here = owners_ref[index] == group_ref[0]
        owns_one = jnp.logical_or(owns_one, here)
        chosen = chosen + jnp.where(here, index, 0)
    fetch_momentum.wait()
    for block in range(blocks):
        part, inner = block // (CHUNK // 128), block % (CHUNK // 128)
        if inner == 0:
            fetch(part).wait()
        wide = grads_ref[part, :, :, inner * 128 : (inner + 1) * 128].astype(f32)
        wide_ref[block, : OWN * MATS, :] = wide.reshape(OWN * MATS, 128)
        gradient = wide_ref[block, pl.ds(chosen, PAD, stride=MATS), :]
        held_state = momentum_ref[pl.ds(block, PAD, stride=blocks), :]
        renewed = jnp.where(owns_one, MOMENTUM_BETA * held_state + gradient, held_state)
        steered = gradient + MOMENTUM_BETA * renewed
        steered_ref[block * STEM : (block + 1) * STEM, :] = steered[:STEM]
        first = blocks * STEM + block * TAIL
        steered_ref[first : first + TAIL, :] = steered[STEM:OWN]


def renew_kernel(
    group_ref, owners_hbm, grads_hbm, momentum_hbm, steered_hbm, renewed_ref,
    owners_ref, grads_ref, momentum_ref, wide_ref, fresh_ref, sems,
):
    blocks = COLS // 128
    chunks = COLS // CHUNK

    def fetch(part):
        lanes = pl.ds(part * CHUNK, CHUNK)
        return pltpu.make_async_copy(grads_hbm.at[:, :, lanes], grads_ref.at[part], sems.at[part])

    fetch_owners = pltpu.make_async_copy(owners_hbm, owners_ref, sems.at[chunks])
    held_rows = pl.ds(0, OWN * blocks)
    fetch_momentum = pltpu.make_async_copy(momentum_hbm, momentum_ref.at[held_rows], sems.at[chunks + 1])
    fetch_owners.start()
    fetch_momentum.start()
    for part in range(chunks):
        fetch(part).start()
    fetch_owners.wait()
    owns_one = owners_ref[0] == group_ref[0]
    chosen = 0
    for index in range(1, MATS):
        here = owners_ref[index] == group_ref[0]
        owns_one = jnp.logical_or(owns_one, here)
        chosen = chosen + jnp.where(here, index, 0)
    fetch_momentum.wait()
    for block in range(blocks):
        part, inner = block // (CHUNK // 128), block % (CHUNK // 128)
        if inner == 0:
            fetch(part).wait()
        wide = grads_ref[part, :, :, inner * 128 : (inner + 1) * 128].astype(f32)
        wide_ref[block, : OWN * MATS, :] = wide.reshape(OWN * MATS, 128)
        gradient = wide_ref[block, pl.ds(chosen, PAD, stride=MATS), :]
        held_state = momentum_ref[pl.ds(block, PAD, stride=blocks), :]
        renewed = jnp.where(owns_one, MOMENTUM_BETA * held_state + gradient, held_state)
        fresh_ref[pl.ds(block, PAD, stride=blocks), :] = renewed
    renewed_ref[...] = fresh_ref[: OWN * blocks, :]


def in_hbm(value):
    return pltpu.with_memory_space_constraint(value, pltpu.HBM)


def read_scratch(*more):
    chunks = COLS // CHUNK
    return [
        pltpu.SMEM((MATS,), jnp.int32),
        pltpu.VMEM((chunks, OWN, MATS, CHUNK), bf16),
        pltpu.VMEM((PAD * COLS // 128, 128), f32),
        pltpu.VMEM((COLS // 128, PAD * MATS, 128), f32),
        *more,
        pltpu.SemaphoreType.DMA((chunks + 2,)),
    ]


def steer(owners, group, grads, momentum):
    return pl.pallas_call(
        steer_kernel,
        in_specs=[pl.BlockSpec(memory_space=pltpu.SMEM)] + [pl.BlockSpec(memory_space=pltpu.HBM)] * 3,
        out_specs=pl.BlockSpec(memory_space=pltpu.VMEM),
        out_shape=jax.ShapeDtypeStruct((OWN * COLS // 128, 128), f32),
        scratch_shapes=read_scratch(),
        compiler_params=pltpu.CompilerParams(vmem_limit_bytes=32 * 1024 * 1024),
    )(group, in_hbm(owners), in_hbm(grads), in_hbm(momentum))


def renew(owners, group, grads, momentum, steered):
    return pl.pallas_call(
        renew_kernel,
        in_specs=[pl.BlockSpec(memory_space=pltpu.SMEM)]
        + [pl.BlockSpec(memory_space=pltpu.HBM)] * 3
        + [pl.BlockSpec(memory_space=pl.ANY)],
        out_specs=pl.BlockSpec(memory_space=pltpu.VMEM),
        out_shape=jax.ShapeDtypeStruct((OWN * COLS // 128, 128), f32),
        scratch_shapes=read_scratch(pltpu.VMEM((PAD * COLS // 128, 128), f32)),
        compiler_params=pltpu.CompilerParams(vmem_limit_bytes=32 * 1024 * 1024),
    )(group, in_hbm(owners), in_hbm(grads), in_hbm(momentum), steered)


def deliver(pieces, owners):
    arrived = lax.all_to_all(pieces, "rep", split_axis=0, concat_axis=0, tiled=True)
    copies = choose(owners, arrived)
    parts = lax.all_to_all(copies, "rep", split_axis=0, concat_axis=0, tiled=True, axis_index_groups=teams())
    rows = assemble(parts.reshape(SHARE, TALL_PIECE, MATS, 128))
    return rows.transpose(1, 0, 2)


def shards(grads, momentum, owners):
    group = lax.axis_index("rep").astype(jnp.int32)[None]
    position = lax.axis_index("fsdp").astype(jnp.int32)[None]
    flat = momentum.reshape(OWN * COLS // 128, 128)
    by_row = grads.transpose(1, 0, 2)
    steered = steer(owners, group, by_row, flat)
    renewed = renew(owners, group, by_row, flat, steered)
    whole = lax.all_gather(steered, "fsdp")
    pieces = orthogonal_rows(position, in_hbm(whole), renewed)
    update = deliver(pieces, owners)
    return (update, renewed.reshape(1, OWN, COLS))


def solution(mesh):
    in_specs = (P(None, "fsdp", None), P("rep", "fsdp", None), P())
    out_specs = (P(None, "fsdp", None), P("rep", "fsdp", None))
    return jax.shard_map(shards, mesh=mesh, in_specs=in_specs, out_specs=out_specs, check_vma=False)
```
